32 devices in a mesh: dp: 8 (over z, core), ctx: 4 (over y, x).
Axes of the slice: x: 2, y: 2, z: 4, core: 2. Of those that a mesh axis runs over, the one named last changes fastest.
Arguments:
- residual_in: bfloat16 [8, 1024, 2048], P('dp', 'ctx'), may hold values from -6 to 6
- document_ids: int32 [8, 1024], P('dp', 'ctx'), may hold values from 0 to 8191, as said below
- attention_gain: bfloat16 [2048], P(('dp', 'ctx')), may hold values from 0.099609375 to 1.8984375
- attention_shift: bfloat16 [2048], P(('dp', 'ctx')), may hold values from -3 to 3
- query_key_value: bfloat16 [2048, 6144], P(('dp', 'ctx')), may hold values from -0.125 to 0.125
- query_value_bias: bfloat16 [4096], P(('dp', 'ctx')), may hold values from -3 to 3
- output_weight: bfloat16 [2048, 2048], P(('dp', 'ctx')), may hold values from -0.5 to 0.5
- output_bias: bfloat16 [2048], P(('dp', 'ctx')), may hold values from -3 to 3
- feedforward_gain: bfloat16 [2048], P(('dp', 'ctx')), may hold values from 0.099609375 to 1.8984375
- feedforward_shift: bfloat16 [2048], P(('dp', 'ctx')), may hold values from -3 to 3
- expand_weight: bfloat16 [2048, 8192], P(('dp', 'ctx')), may hold values from -0.125 to 0.125
- expand_bias: bfloat16 [8192], P(('dp', 'ctx')), may hold values from -3 to 3
- contract_weight: bfloat16 [8192, 2048], P(('dp', 'ctx')), may hold values from -0.09375 to 0.09375
- contract_bias: bfloat16 [2048], P(('dp', 'ctx')), may hold values from -3 to 3
- output_grad: bfloat16 [8, 1024, 2048], P('dp', 'ctx'), may hold values from -6 to 6
Outputs:
- layer_output: bfloat16 [8, 1024, 2048], P('dp', 'ctx')
- input_grad: bfloat16 [8, 1024, 2048], P('dp', 'ctx')
- attention_gain_grad: float32 [2048], P(('dp', 'ctx'))
- attention_shift_grad: float32 [2048], P(('dp', 'ctx'))
- query_key_value_grad: float32 [2048, 6144], P(('dp', 'ctx'))
- query_value_bias_grad: float32 [4096], P(('dp', 'ctx'))
- output_weight_grad: float32 [2048, 2048], P(('dp', 'ctx'))
- output_bias_grad: float32 [2048], P(('dp', 'ctx'))
- feedforward_gain_grad: float32 [2048], P(('dp', 'ctx'))
- feedforward_shift_grad: float32 [2048], P(('dp', 'ctx'))
- expand_weight_grad: float32 [2048, 8192], P(('dp', 'ctx'))
- expand_bias_grad: float32 [8192], P(('dp', 'ctx'))
- contract_weight_grad: float32 [8192, 2048], P(('dp', 'ctx'))
- contract_bias_grad: float32 [2048], P(('dp', 'ctx'))
The draws below stay inside these ranges and needn't reach their ends.
Inputs may be any that keep to these rules, and one draw needn't show every extreme that they name: document_ids[b, p] = b * 1024 + s, where s is the first position of the document that holds position p of sequence b; every document is a run of consecutive positions of one sequence, so values stay below 8192.
All inputs are finite; a program needn't handle non-finite values.
Results may differ from the reference program's by a relative error of at most 0.013.
Values may be sent and summed in bfloat16 or wider, within the bound.
No kernel may reach another device: no remote copies, remote signals or barrier semaphores. Data moves between devices by JAX's collectives and lax.ppermute only.
A program may use at most 512 MiB of HBM per device.

```python
import jax
import jax.numpy as jnp
from jax import lax

D = 2048
HEADS = 32
HEAD_DIM = 64
FF = 8192
SEQS = 1
STRETCH = 256
SEQ_LEN = 1024
BATCH = 8


def draw_document_ids(key, part):
    length = SEQ_LEN
    batch = BATCH
    spacing = max(SEQ_LEN // 4, 2)
    pieces = jax.random.split(jax.random.fold_in(key, 11), 4)
    place = jnp.arange(length, dtype=jnp.int32)
    cuts = jax.random.randint(pieces[0], (batch, length), 0, spacing) == 0
    cuts = cuts | (place[None, :] == 0)
    first = jax.random.randint(pieces[1], (batch, 1), 0, STRETCH)
    last = jax.random.randint(pieces[2], (batch, 1), length - STRETCH, length)
    chosen = jax.random.randint(pieces[3], (batch // SEQS, 1), 0, SEQS)
    rows = jnp.arange(batch, dtype=jnp.int32)[:, None]
    spanning = rows % SEQS == jnp.repeat(chosen, SEQS, axis=0)
    inside = (place[None, :] > first) & (place[None, :] <= last)
    cuts = jnp.where(spanning & inside, False, cuts)
    cuts = jnp.where(spanning & (place[None, :] == first), True, cuts)
    cuts = jnp.where(spanning & (place[None, :] == last + 1), True, cuts)
    starts = lax.cummax(jnp.where(cuts, place[None, :], 0), axis=1)
    return (starts + rows * length).astype(jnp.int32)


def steps_of(rng, dims, cuts, low, largest):
    level, own = 1.0, jax.random.fold_in(rng, 6)
    for position, parts in cuts:
        heights = jnp.exp(jax.random.uniform(jax.random.fold_in(own, position), (parts,), jnp.float32, low / len(cuts), largest / len(cuts)))
        level = level * jnp.repeat(heights, dims[position] // parts).reshape([-1 if axis == position else 1 for axis in range(len(dims))])
    return level


def gaussian(key, extent, deviation, reach, shards=(), kind=jnp.bfloat16):
    level = steps_of(key, extent, shards, -0.22, 0.18) if shards else 1.0
    values = jax.random.normal(key, extent, jnp.float32) * deviation * level
    return jnp.minimum(jnp.maximum(values, -reach), reach).astype(kind)


def setup_inputs(seed: int = 0) -> dict:
    key_list = jax.random.split(jax.random.key(seed), 16)
    return {
        "residual_in": gaussian(key_list[0], (BATCH, SEQ_LEN, D), 1.0, 6.0, ((0, 8), (1, 4))),
        "document_ids": draw_document_ids(jax.random.fold_in(key_list[15], 71), 0),
        "attention_gain": jnp.clip(1.0 + 0.18 * jax.random.normal(key_list[2], (D,), jnp.float32), 0.099609375, 1.8984375).astype(jnp.bfloat16),
        "attention_shift": gaussian(key_list[3], (D,), 0.5, 3.0, ((0, 32),)),
        "query_key_value": gaussian(key_list[4], (D, 3 * D), D ** -0.5, 0.125, ((0, 32),)),
        "query_value_bias": gaussian(key_list[5], (2 * D,), 0.5, 3.0, ((0, 32),)),
        "output_weight": gaussian(key_list[6], (D, D), (D // 16) ** -0.5, 0.5, ((0, 32),)),
        "output_bias": gaussian(key_list[7], (D,), 0.5, 3.0, ((0, 32),)),
        "feedforward_gain": jnp.clip(1.0 + 0.18 * jax.random.normal(key_list[8], (D,), jnp.float32), 0.099609375, 1.8984375).astype(jnp.bfloat16),
        "feedforward_shift": gaussian(key_list[9], (D,), 0.5, 3.0, ((0, 32),)),
        "expand_weight": gaussian(key_list[10], (D, FF), D ** -0.5, 0.125, ((0, 32),)),
        "expand_bias": gaussian(key_list[11], (FF,), 0.5, 3.0, ((0, 32),)),
        "contract_weight": gaussian(key_list[12], (FF, D), (FF // 2) ** -0.5, 0.09375, ((0, 32),)),
        "contract_bias": gaussian(key_list[13], (D,), 0.5, 3.0, ((0, 32),)),
        "output_grad": gaussian(key_list[14], (BATCH, SEQ_LEN, D), 1.0, 6.0, ((0, 8), (1, 4))),
    }


@jax.custom_vjp
def low(v):
    return lax.optimization_barrier(v.astype(jnp.bfloat16)).astype(jnp.float32)

@jax.custom_vjp
def low_back(v):
    return v

def low_keep(v):
    return (low(v), None)

def low_pass(kept, grad):
    return (grad,)

def back_keep(v):
    return (v, None)

def back_low(kept, grad):
    return (low(grad),)
low.defvjp(low_keep, low_pass)
low_back.defvjp(back_keep, back_low)
epsilon = 1e-05

def layer_norm(value, gain, shift):
    mean = lax.optimization_barrier(jnp.mean(value, axis=-1, keepdims=True))
    centred = value - mean
    scale = lax.rsqrt(lax.optimization_barrier(jnp.mean(centred * centred, axis=-1, keepdims=True)) + epsilon)
    return centred * scale * gain + shift

def matmul(left, right):
    return jnp.dot(left, right, preferred_element_type=jnp.float32, precision=lax.Precision.HIGHEST)

def attend(item):
    queries, keys, values, starts = item
    length = queries.shape[0]
    place = jnp.arange(length, dtype=jnp.int32)
    slopes = jnp.exp2(-8.0 * (jnp.arange(HEADS, dtype=jnp.float32) + 1.0) / HEADS)
    products = jnp.einsum('qhd,khd->hqk', queries, keys, precision=lax.Precision.HIGHEST)
    distance = (place[:, None] - place[None, :]).astype(jnp.float32)
    scores = products * 0.125 - slopes[:, None, None] * distance[None]
    visible = (starts[:, None] == starts[None, :]) & (place[None, :] <= place[:, None])
    scores = low_back(jnp.where(visible[None], scores, -1e+30))
    top = lax.optimization_barrier(jnp.max(scores, axis=-1, keepdims=True))
    weights = jnp.exp(scores - top)
    probs = weights / lax.optimization_barrier(jnp.sum(weights, axis=-1, keepdims=True))
    mixed = jnp.einsum('hqk,khd->qhd', low(probs), values, precision=lax.Precision.HIGHEST)
    return mixed.reshape(length, HEADS * HEAD_DIM)

def forward(params, block, starts):
    att_gain, att_shift, qkv_weight, qv_bias, out_weight, out_bias, ff_gain, ff_shift, exp_weight, exp_bias, con_weight, con_bias = params
    rows = block.reshape(-1, D)
    normed = low(layer_norm(rows, att_gain, att_shift))
    projected = matmul(normed, qkv_weight)
    queries = low(low_back(projected[:, :D] + qv_bias[:D]))
    keys = low(low_back(projected[:, D:2 * D]))
    values = low(low_back(projected[:, 2 * D:] + qv_bias[D:]))
    shape = (block.shape[0], block.shape[1], HEADS, HEAD_DIM)
    attended = lax.map(jax.checkpoint(attend), (queries.reshape(shape), keys.reshape(shape), values.reshape(shape), starts))
    attended = low(low_back(attended.reshape(-1, D)))
    branch = low_back(matmul(attended, out_weight) + out_bias)
    middle = rows + branch
    normed_mid = low(layer_norm(middle, ff_gain, ff_shift))
    inner = low_back(matmul(normed_mid, exp_weight) + exp_bias)
    active = low(inner * (1.0 + lax.erf(inner * 0.7071067811865476)) * 0.5)
    result = middle + matmul(active, con_weight) + con_bias
    return result.reshape(block.shape)

def reference(residual_in, document_ids, attention_gain, attention_shift, query_key_value, query_value_bias, output_weight, output_bias, feedforward_gain, feedforward_shift, expand_weight, expand_bias, contract_weight, contract_bias, output_grad):
    params = tuple((item.astype(jnp.float32) for item in (attention_gain, attention_shift, query_key_value, query_value_bias, output_weight, output_bias, feedforward_gain, feedforward_shift, expand_weight, expand_bias, contract_weight, contract_bias)))
    batch = residual_in.shape[0]
    group = 4 if batch % 4 == 0 else 2 if batch % 2 == 0 else 1
    count = batch // group
    blocks = residual_in.astype(jnp.float32).reshape(count, group, SEQ_LEN, D)
    cotangents = output_grad.astype(jnp.float32).reshape(count, group, SEQ_LEN, D)
    documents = document_ids.astype(jnp.int32).reshape(count, group, SEQ_LEN)

    def accumulate(totals, item):
        block, cotangent, starts = item

        def apply(weights, inputs):
            return forward(weights, inputs, starts)
        result, pullback = jax.vjp(apply, params, block)
        weight_grads, block_grad = pullback(cotangent)
        return (jax.tree.map(jnp.add, totals, weight_grads), (result, block_grad))
    zeros = jax.tree.map(jnp.zeros_like, params)
    totals, (results, grads) = lax.scan(accumulate, zeros, (blocks, cotangents, documents))
    shape = residual_in.shape
    return (results.reshape(shape).astype(jnp.bfloat16), grads.reshape(shape).astype(jnp.bfloat16), totals[0], totals[1], totals[2], totals[3], totals[4], totals[5], totals[6], totals[7], totals[8], totals[9], totals[10], totals[11])
```

```python
import jax
import jax.numpy as jnp
from jax import lax
from jax.experimental import pallas as pl
from jax.experimental.pallas import tpu as pltpu
from jax.sharding import PartitionSpec as P

HEADS = 32
HEAD_DIM = 64
PAIR = 2 * HEAD_DIM

bf16 = jnp.bfloat16
f32 = jnp.float32
epsilon = 1e-05


def unit_rows(value):
    mean = jnp.mean(value, axis=-1, keepdims=True)
    centred = value - mean
    scale = lax.rsqrt(jnp.mean(centred * centred, axis=-1, keepdims=True) + epsilon)
    return centred * scale, scale


def norm_backward(grad, unit, scale, gain):
    scaled = grad * gain
    level = jnp.mean(scaled, axis=-1, keepdims=True)
    along = jnp.mean(scaled * unit, axis=-1, keepdims=True)
    return (
        scale * (scaled - level - unit * along),
        jnp.sum(grad * unit, axis=0),
        jnp.sum(grad, axis=0),
    )


def dot(left, right, contract=((1,), (0,))):
    return lax.dot_general(left, right, (contract, ((), ())), preferred_element_type=f32)


def lane_mask(half):
    lane = lax.broadcasted_iota(jnp.int32, (1, PAIR), 1)
    return (lane >= HEAD_DIM) if half else (lane < HEAD_DIM)


def attend_forward_kernel(slope_ref, start_ref, q_ref, k_ref, v_ref, out_ref, probs_ref):
    length = q_ref.shape[0]
    block = min(256, length)
    pair = pl.program_id(0)
    for index in range(length // block):
        rows = pl.ds(index * block, block)
        span = (index + 1) * block
        starts = start_ref[rows, :]
        q_place = index * block + lax.broadcasted_iota(jnp.int32, (block, span), 0)
        k_place = lax.broadcasted_iota(jnp.int32, (block, span), 1)
        visible = (k_place >= starts) & (k_place <= q_place)
        k_row = lax.broadcasted_iota(jnp.int32, (1, span), 1).astype(f32)
        mixed = []
        for half in range(2):
            slope = slope_ref[pair * 2 + half]
            query = jnp.where(lane_mask(half), q_ref[rows, :] * bf16(0.125), bf16(0))
            scores = dot(query, k_ref[:span, :], ((1,), (1,))) + slope * k_row
            scores = jnp.where(visible, scores, -1e30)
            top = jnp.max(scores, axis=-1, keepdims=True)
            weights = jnp.exp(scores - top)
            total = jnp.sum(weights, axis=-1, keepdims=True)
            probs = (weights * (1.0 / total)).astype(bf16)
            probs_ref[half, rows, :span] = probs
            mixed.append(dot(probs, v_ref[:span, :]))
        out_ref[rows, :] = jnp.where(lane_mask(0), mixed[0], mixed[1]).astype(bf16)


def attend_backward_kernel(probs_ref, q_ref, k_ref, v_ref, g_ref, dq_ref, dk_ref, dv_ref, dk_sum, dv_sum):
    length = q_ref.shape[0]
    block = min(256, length)
    dk_sum[...] = jnp.zeros_like(dk_sum)
    dv_sum[...] = jnp.zeros_like(dv_sum)
    for index in range(length // block):
        rows = pl.ds(index * block, block)
        span = (index + 1) * block
        parts = []
        for half in range(2):
            mask = lane_mask(half)
            grad = jnp.where(mask, g_ref[rows, :], bf16(0))
            query = jnp.where(mask, q_ref[rows, :] * bf16(0.125), bf16(0))
            probs_low = probs_ref[half, rows, :span]
            probs = probs_low.astype(f32)
            grad_probs = dot(grad, v_ref[:span, :], ((1,), (1,)))
            along = jnp.sum(probs * grad_probs, axis=-1, keepdims=True)
            grad_scores = (probs * (grad_probs - along)).astype(bf16)
            parts.append(dot(grad_scores, k_ref[:span, :]))
            dk_sum[:span, :] += dot(grad_scores, query, ((0,), (0,)))
            dv_sum[:span, :] += dot(probs_low, grad, ((0,), (0,)))
        dq_ref[rows, :] = (jnp.where(lane_mask(0), parts[0], parts[1]) * 0.125).astype(bf16)
    dk_ref[...] = dk_sum[...].astype(bf16)
    dv_ref[...] = dv_sum[...].astype(bf16)


def attend_forward(slopes, starts, projected):
    length = projected.shape[0]
    heads = projected.shape[1] // (3 * HEAD_DIM)
    pairs = heads // 2
    column = lambda first: pl.BlockSpec((length, PAIR), lambda p: (0, first + p))
    return pl.pallas_call(
        attend_forward_kernel,
        grid=(pairs,),
        in_specs=[
            pl.BlockSpec(memory_space=pltpu.SMEM),
            pl.BlockSpec((length, 1), lambda p: (0, 0)),
            column(0),
            column(pairs),
            column(2 * pairs),
        ],
        out_specs=[column(0), pl.BlockSpec((2, length, length), lambda p: (p, 0, 0))],
        out_shape=[
            jax.ShapeDtypeStruct((length, heads * HEAD_DIM), bf16),
            jax.ShapeDtypeStruct((heads, length, length), bf16),
        ],
        compiler_params=pltpu.CompilerParams(vmem_limit_bytes=50 * 2**20),
        cost_estimate=pl.CostEstimate(
            flops=4 * heads * length * length * PAIR,
            bytes_accessed=2 * heads * length * length,
            transcendentals=heads * length * length,
        ),
        name="attend_forward",
    )(slopes, starts, projected, projected, projected)


def attend_backward(probs, projected, grad):
    length = projected.shape[0]
    heads = projected.shape[1] // (3 * HEAD_DIM)
    pairs = heads // 2
    column = lambda first: pl.BlockSpec((length, PAIR), lambda p: (0, first + p))
    shape = jax.ShapeDtypeStruct((length, heads * HEAD_DIM), bf16)
    return pl.pallas_call(
        attend_backward_kernel,
        grid=(pairs,),
        in_specs=[
            pl.BlockSpec((2, length, length), lambda p: (p, 0, 0)),
            column(0),
            column(pairs),
            column(2 * pairs),
            column(0),
        ],
        out_specs=[column(0), column(0), column(0)],
        out_shape=[shape, shape, shape],
        scratch_shapes=[pltpu.VMEM((length, PAIR), f32), pltpu.VMEM((length, PAIR), f32)],
        compiler_params=pltpu.CompilerParams(vmem_limit_bytes=50 * 2**20),
        cost_estimate=pl.CostEstimate(
            flops=8 * heads * length * length * PAIR,
            bytes_accessed=2 * heads * length * length,
            transcendentals=0,
        ),
        name="attend_backward",
    )(probs, projected, projected, projected, grad)


ALL = ("dp", "ctx")


def swap(value):
    return lax.all_to_all(value, "ctx", 0, 0, tiled=True)


def shards(
    residual_in,
    document_ids,
    attention_gain,
    attention_shift,
    query_key_value,
    query_value_bias,
    output_weight,
    output_bias,
    feedforward_gain,
    feedforward_shift,
    expand_weight,
    expand_bias,
    contract_weight,
    contract_bias,
    output_grad,
):
    groups, ways = lax.axis_size("dp"), lax.axis_size("ctx")
    me_dp, me = lax.axis_index("dp"), lax.axis_index("ctx")
    seqs, stretch, width = residual_in.shape
    assert seqs == 1
    length = stretch * ways
    slab = query_key_value.shape[0]
    inner_slab = contract_weight.shape[0]
    features = width // ways
    heads = HEADS // ways

    def gather_ctx(value):
        return lax.all_gather(value, "ctx", axis=0, tiled=True)

    def scatter_ctx(value):
        return lax.psum_scatter(value.astype(bf16), "ctx", scatter_dimension=0, tiled=True).astype(f32)

    def gather_dp(value):
        return lax.all_gather(value, "dp", axis=0, tiled=True)

    def scatter_dp(value):
        return lax.psum_scatter(value.astype(bf16), "dp", scatter_dimension=0, tiled=True)

    small = (
        attention_gain,
        attention_shift,
        output_bias,
        feedforward_gain,
        feedforward_shift,
        contract_bias,
        query_value_bias,
        expand_bias,
    )
    packed = lax.all_gather(jnp.concatenate(small), ALL, axis=0).astype(f32)
    whole, at = [], 0
    for item in small:
        whole.append(packed[:, at : at + item.shape[0]].reshape(-1))
        at += item.shape[0]
    att_gain, att_shift, out_bias, ff_gain, ff_shift, con_bias, qv_bias, exp_bias = whole
    exp_bias = lax.dynamic_index_in_dim(
        exp_bias.reshape(groups, ways, inner_slab), me, 1, keepdims=False
    ).reshape(-1)
    qv_bias = lax.dynamic_index_in_dim(qv_bias.reshape(2, ways, features), me, 1, keepdims=False)

    qkv_rows = query_key_value.reshape(slab, 3, ways, features).transpose(2, 0, 1, 3)
    qkv_weight = gather_dp(swap(qkv_rows.reshape(ways * slab, 3 * features)))
    out_weight = lax.all_gather(output_weight, ALL, axis=0, tiled=True)
    exp_rows = expand_weight.reshape(slab, groups, ways, inner_slab).transpose(2, 0, 1, 3)
    exp_weight = gather_dp(swap(exp_rows.reshape(ways * slab, groups * inner_slab)))
    con_weight = gather_dp(contract_weight)

    block = residual_in[0]
    block_all = gather_ctx(block)
    grad_out = output_grad[0]
    grad_out_all = gather_ctx(grad_out)
    docs_all = gather_ctx(document_ids[0])
    starts = (docs_all - me_dp * length)[:, None]
    slopes = jnp.exp2(
        -8.0 * ((me * heads + jnp.arange(heads, dtype=jnp.int32)).astype(f32) + 1.0) / HEADS
    )

    rows = block.astype(f32)
    unit_in, scale_in = unit_rows(rows)
    normed_low = (unit_rows(block_all.astype(f32))[0] * att_gain + att_shift).astype(bf16)
    bias = jnp.concatenate([qv_bias[0], jnp.zeros((features,), f32), qv_bias[1]])
    projected = (dot(normed_low, qkv_weight) + bias).astype(bf16)
    attended, probs = attend_forward(slopes, starts, projected)
    attended_rows = lax.all_to_all(attended, "ctx", 0, 1, tiled=True)
    middle = rows + dot(attended_rows, out_weight) + out_bias

    unit_mid, scale_mid = unit_rows(middle)
    normed_mid = gather_ctx((unit_mid * ff_gain + ff_shift).astype(bf16))
    inner = dot(normed_mid, exp_weight) + exp_bias
    cumulative = (1.0 + lax.erf(inner * 0.7071067811865476)) * 0.5
    active = (inner * cumulative).astype(bf16)
    result = middle + scatter_ctx(dot(active, con_weight)) + con_bias
    layer_output = result.astype(bf16)[None]

    con_grad = scatter_dp(dot(active, grad_out_all, ((0,), (0,)))).astype(f32)
    grad_active = dot(grad_out_all, con_weight, ((1,), (1,)))
    density = jnp.exp(-0.5 * inner * inner) * 0.3989422804014327
    grad_inner = (grad_active * (cumulative + inner * density)).astype(bf16)
    exp_grad = swap(scatter_dp(dot(normed_mid, grad_inner, ((0,), (0,)))))
    exp_grad = (
        exp_grad.reshape(ways, slab, groups, inner_slab)
        .transpose(1, 2, 0, 3)
        .reshape(slab, -1)
        .astype(f32)
    )
    exp_bias_term = jnp.sum(grad_inner.astype(f32), axis=0)
    grad_normed_mid = scatter_ctx(dot(grad_inner, exp_weight, ((1,), (1,))))
    grad_mid_norm, ff_gain_term, ff_shift_term = norm_backward(
        grad_normed_mid, unit_mid, scale_mid, ff_gain
    )
    grad_out_full = grad_out.astype(f32)
    grad_middle = grad_out_full + grad_mid_norm
    grad_branch = grad_middle.astype(bf16)

    grad_attended = dot(grad_branch, out_weight, ((1,), (1,))).astype(bf16)
    grad_heads = lax.all_to_all(grad_attended, "ctx", 1, 0, tiled=True)
    grad_projected = jnp.concatenate(attend_backward(probs, projected, grad_heads), axis=1)
    out_grad = lax.psum_scatter(
        dot(attended_rows, grad_branch, ((0,), (0,))).astype(bf16),
        ALL,
        scatter_dimension=0,
        tiled=True,
    ).astype(f32)
    grad_normed_in = scatter_ctx(dot(grad_projected, qkv_weight, ((1,), (1,))))
    qkv_grad = swap(scatter_dp(dot(normed_low, grad_projected, ((0,), (0,)))))
    qkv_grad = (
        qkv_grad.reshape(ways, slab, 3, features)
        .transpose(1, 2, 0, 3)
        .reshape(slab, -1)
        .astype(f32)
    )
    grad_in_norm, att_gain_term, att_shift_term = norm_backward(
        grad_normed_in, unit_in, scale_in, att_gain
    )
    input_grad = (grad_middle + grad_in_norm).astype(bf16)[None]

    bias_sums = jnp.sum(grad_projected.astype(f32), axis=0).reshape(3, features)
    qv_term = lax.dynamic_update_slice(
        jnp.zeros((2, ways, features), f32),
        jnp.stack([bias_sums[0], bias_sums[2]])[:, None],
        (0, me, 0),
    ).reshape(-1)
    exp_term = lax.dynamic_update_slice(
        jnp.zeros((groups, ways, inner_slab), f32),
        exp_bias_term.reshape(groups, 1, inner_slab),
        (0, me, 0),
    ).reshape(-1)
    terms = (
        att_gain_term,
        att_shift_term,
        jnp.sum(grad_branch.astype(f32), axis=0),
        ff_gain_term,
        ff_shift_term,
        jnp.sum(grad_out_full, axis=0),
        qv_term,
        exp_term,
    )
    count = groups * ways
    sums = lax.psum_scatter(
        jnp.concatenate([item.reshape(count, -1) for item in terms], axis=1),
        ALL,
        scatter_dimension=0,
        tiled=True,
    ).reshape(-1)
    own, at = [], 0
    for item in small:
        own.append(sums[at : at + item.shape[0]])
        at += item.shape[0]
    return (
        layer_output,
        input_grad,
        own[0],
        own[1],
        qkv_grad,
        own[6],
        out_grad,
        own[2],
        own[3],
        own[4],
        exp_grad,
        own[7],
        con_grad,
        own[5],
    )


def solution(mesh):
    tokens = P("dp", "ctx", None)
    vector = P(ALL)
    matrix = P(ALL, None)
    in_specs = (
        tokens,
        P("dp", "ctx"),
        vector,
        vector,
        matrix,
        vector,
        matrix,
        vector,
        vector,
        vector,
        matrix,
        vector,
        matrix,
        vector,
        tokens,
    )
    out_specs = (
        tokens,
        tokens,
        vector,
        vector,
        matrix,
        vector,
        matrix,
        vector,
        vector,
        vector,
        matrix,
        vector,
        matrix,
        vector,
    )
    return jax.shard_map(shards, mesh=mesh, in_specs=in_specs, out_specs=out_specs, check_vma=False)
```

```python
import functools

import jax
import jax.numpy as jnp
from jax import lax
from jax.experimental import pallas as pl
from jax.experimental.pallas import tpu as pltpu
from jax.sharding import PartitionSpec as P

HEADS = 32
HEAD_DIM = 64
PAIR = 2 * HEAD_DIM

bf16 = jnp.bfloat16
f32 = jnp.float32
epsilon = 1e-05


def unit_rows(value):
    mean = jnp.mean(value, axis=-1, keepdims=True)
    centred = value - mean
    scale = lax.rsqrt(jnp.mean(centred * centred, axis=-1, keepdims=True) + epsilon)
    return centred * scale, scale


def norm_backward(grad, unit, scale, gain):
    scaled = grad * gain
    level = jnp.mean(scaled, axis=-1, keepdims=True)
    along = jnp.mean(scaled * unit, axis=-1, keepdims=True)
    return (
        scale * (scaled - level - unit * along),
        jnp.sum(grad * unit, axis=0),
        jnp.sum(grad, axis=0),
    )


def dot(left, right, contract=((1,), (0,))):
    return lax.dot_general(left, right, (contract, ((), ())), preferred_element_type=f32)


def lane_mask(half):
    lane = lax.broadcasted_iota(jnp.int32, (1, PAIR), 1)
    return (lane >= HEAD_DIM) if half else (lane < HEAD_DIM)


def stretch_rows(me_ref, index, block):
    return pl.ds(pl.multiple_of((index ^ me_ref[0]) * block, block), block)


def in_order(me_ref, source, target, block):
    for index in range(source.shape[0] // block):
        target[pl.ds(index * block, block), :] = source[stretch_rows(me_ref, index, block), :]


def attend_forward_kernel(
    block, me_ref, slope_ref, start_ref, q_ref, k_in, v_in, out_ref, probs_ref, k_ref, v_ref
):
    length = q_ref.shape[0]
    pair = pl.program_id(0)
    in_order(me_ref, k_in, k_ref, block)
    in_order(me_ref, v_in, v_ref, block)
    for index in range(length // block):
        rows = stretch_rows(me_ref, index, block)
        place = pl.ds(index * block, block)
        span = (index + 1) * block
        starts = start_ref[rows, :]
        q_place = index * block + lax.broadcasted_iota(jnp.int32, (block, span), 0)
        k_place = lax.broadcasted_iota(jnp.int32, (block, span), 1)
        visible = (k_place >= starts) & (k_place <= q_place)
        k_row = lax.broadcasted_iota(jnp.int32, (1, span), 1).astype(f32)
        mixed = []
        for half in range(2):
            slope = slope_ref[pair * 2 + half]
            query = jnp.where(lane_mask(half), q_ref[rows, :] * bf16(0.125), bf16(0))
            scores = dot(query, k_ref[:span, :], ((1,), (1,))) + slope * k_row
            scores = jnp.where(visible, scores, -1e30)
            top = jnp.max(scores, axis=-1, keepdims=True)
            weights = jnp.exp(scores - top)
            total = jnp.sum(weights, axis=-1, keepdims=True)
            probs = (weights * (1.0 / total)).astype(bf16)
            probs_ref[half, place, :span] = probs
            mixed.append(dot(probs, v_ref[:span, :]))
        out_ref[rows, :] = jnp.where(lane_mask(0), mixed[0], mixed[1]).astype(bf16)


def attend_backward_kernel(
    block, me_ref, probs_ref, q_ref, k_in, v_in, g_ref, dq_ref, dk_ref, dv_ref, k_ref, v_ref, dk_sum, dv_sum
):
    length = q_ref.shape[0]
    in_order(me_ref, k_in, k_ref, block)
    in_order(me_ref, v_in, v_ref, block)
    dk_sum[...] = jnp.zeros_like(dk_sum)
    dv_sum[...] = jnp.zeros_like(dv_sum)
    for index in range(length // block):
        rows = stretch_rows(me_ref, index, block)
        place = pl.ds(index * block, block)
        span = (index + 1) * block
        parts = []
        for half in range(2):
            mask = lane_mask(half)
            grad = jnp.where(mask, g_ref[rows, :], bf16(0))
            query = jnp.where(mask, q_ref[rows, :] * bf16(0.125), bf16(0))
            probs_low = probs_ref[half, place, :span]
            probs = probs_low.astype(f32)
            grad_probs = dot(grad, v_ref[:span, :], ((1,), (1,)))
            along = jnp.sum(probs * grad_probs, axis=-1, keepdims=True)
            grad_scores = (probs * (grad_probs - along)).astype(bf16)
            parts.append(dot(grad_scores, k_ref[:span, :]))
            dk_sum[:span, :] += dot(grad_scores, query, ((0,), (0,)))
            dv_sum[:span, :] += dot(probs_low, grad, ((0,), (0,)))
        dq_ref[rows, :] = (jnp.where(lane_mask(0), parts[0], parts[1]) * 0.125).astype(bf16)
    for index in range(length // block):
        rows = stretch_rows(me_ref, index, block)
        place = pl.ds(index * block, block)
        dk_ref[rows, :] = dk_sum[place, :].astype(bf16)
        dv_ref[rows, :] = dv_sum[place, :].astype(bf16)


def attend_forward(block, me, slopes, starts, projected):
    length = projected.shape[0]
    heads = projected.shape[1] // (3 * HEAD_DIM)
    pairs = heads // 2
    column = lambda first: pl.BlockSpec((length, PAIR), lambda p: (0, first + p))
    return pl.pallas_call(
        functools.partial(attend_forward_kernel, block),
        grid=(pairs,),
        in_specs=[
            pl.BlockSpec(memory_space=pltpu.SMEM),
            pl.BlockSpec(memory_space=pltpu.SMEM),
            pl.BlockSpec((length, 1), lambda p: (0, 0)),
            column(0),
            column(pairs),
            column(2 * pairs),
        ],
        out_specs=[column(0), pl.BlockSpec((2, length, length), lambda p: (p, 0, 0))],
        out_shape=[
            jax.ShapeDtypeStruct((length, heads * HEAD_DIM), bf16),
            jax.ShapeDtypeStruct((heads, length, length), bf16),
        ],
        scratch_shapes=[pltpu.VMEM((length, PAIR), bf16), pltpu.VMEM((length, PAIR), bf16)],
        compiler_params=pltpu.CompilerParams(vmem_limit_bytes=50 * 2**20),
        cost_estimate=pl.CostEstimate(
            flops=4 * heads * length * length * PAIR,
            bytes_accessed=2 * heads * length * length,
            transcendentals=heads * length * length,
        ),
        name="attend_forward",
    )(me, slopes, starts, projected, projected, projected)


def attend_backward(block, me, probs, projected, grad):
    length = projected.shape[0]
    heads = projected.shape[1] // (3 * HEAD_DIM)
    pairs = heads // 2
    column = lambda first: pl.BlockSpec((length, PAIR), lambda p: (0, first + p))
    shape = jax.ShapeDtypeStruct((length, heads * HEAD_DIM), bf16)
    return pl.pallas_call(
        functools.partial(attend_backward_kernel, block),
        grid=(pairs,),
        in_specs=[
            pl.BlockSpec(memory_space=pltpu.SMEM),
            pl.BlockSpec((2, length, length), lambda p: (p, 0, 0)),
            column(0),
            column(pairs),
            column(2 * pairs),
            column(0),
        ],
        out_specs=[column(0), column(0), column(0)],
        out_shape=[shape, shape, shape],
        scratch_shapes=[
            pltpu.VMEM((length, PAIR), bf16),
            pltpu.VMEM((length, PAIR), bf16),
            pltpu.VMEM((length, PAIR), f32),
            pltpu.VMEM((length, PAIR), f32),
        ],
        compiler_params=pltpu.CompilerParams(vmem_limit_bytes=50 * 2**20),
        cost_estimate=pl.CostEstimate(
            flops=8 * heads * length * length * PAIR,
            bytes_accessed=2 * heads * length * length,
            transcendentals=0,
        ),
        name="attend_backward",
    )(me, probs, projected, projected, projected, grad)


def relative_slabs(value, me, ways, slab):
    width = value.shape[1]
    lane = lax.broadcasted_iota(jnp.int32, (1, width), 1)
    bit = 1
    while bit < ways:
        size = bit * slab
        upper, lower = pltpu.roll(value, size, 1), pltpu.roll(value, width - size, 1)
        swapped = jnp.where((lane & size) != 0, upper, lower)
        value = jnp.where((me & bit) != 0, swapped, value)
        bit *= 2
    return value


def arrange_kernel(slab, spot_ref, *refs):
    *part_refs, own_ref, other_ref, whole = refs
    ways = len(part_refs)
    me, core = spot_ref[0], spot_ref[1]
    features, width = part_refs[0].shape[1], whole.shape[1]
    for way, ref in enumerate(part_refs):
        place = pl.ds(pl.multiple_of((me ^ way) * features, 128), features)
        whole[:, place] = ref[...].astype(f32)
    whole[...] = relative_slabs(whole[...], me, ways, slab)
    size = ways * slab
    for n in range(width // (2 * size)):
        for which, ref in ((0, own_ref), (1, other_ref)):
            place = pl.ds(pl.multiple_of((2 * n + (core ^ which)) * size, 128), size)
            ref[:, n * size : (n + 1) * size] = whole[:, place].astype(bf16)


def disarrange_kernel(slab, spot_ref, own_ref, other_ref, *refs):
    *part_refs, whole = refs
    ways = len(part_refs)
    me, core = spot_ref[0], spot_ref[1]
    features, width = part_refs[0].shape[1], whole.shape[1]
    size = ways * slab
    for n in range(width // (2 * size)):
        for which, ref in ((0, own_ref), (1, other_ref)):
            place = pl.ds(pl.multiple_of((2 * n + (core ^ which)) * size, 128), size)
            whole[:, place] = ref[:, n * size : (n + 1) * size]
    whole[...] = relative_slabs(whole[...], me, ways, slab)
    for way, ref in enumerate(part_refs):
        place = pl.ds(pl.multiple_of((me ^ way) * features, 128), features)
        ref[...] = whole[:, place].astype(bf16)


def arrange(slab, spot, parts):
    rows, features = parts[0].shape
    width = features * len(parts)
    vmem = pl.BlockSpec(memory_space=pltpu.VMEM)
    half = jax.ShapeDtypeStruct((rows, width // 2), bf16)
    return pl.pallas_call(
        functools.partial(arrange_kernel, slab),
        in_specs=[pl.BlockSpec(memory_space=pltpu.SMEM)] + [vmem] * len(parts),
        out_specs=[vmem, vmem],
        out_shape=[half, half],
        scratch_shapes=[pltpu.VMEM((rows, width), f32)],
        compiler_params=pltpu.CompilerParams(vmem_limit_bytes=32 * 2**20),
        cost_estimate=pl.CostEstimate(
            flops=16 * rows * width, bytes_accessed=4 * rows * width, transcendentals=0
        ),
        name="arrange",
    )(spot, *parts)


def disarrange(slab, spot, own, other, ways):
    rows, width = own.shape[0], 2 * own.shape[1]
    vmem = pl.BlockSpec(memory_space=pltpu.VMEM)
    part = jax.ShapeDtypeStruct((rows, width // ways), bf16)
    return pl.pallas_call(
        functools.partial(disarrange_kernel, slab),
        in_specs=[pl.BlockSpec(memory_space=pltpu.SMEM), vmem, vmem],
        out_specs=[vmem] * ways,
        out_shape=[part] * ways,
        scratch_shapes=[pltpu.VMEM((rows, width), f32)],
        compiler_params=pltpu.CompilerParams(vmem_limit_bytes=32 * 2**20),
        cost_estimate=pl.CostEstimate(
            flops=16 * rows * width, bytes_accessed=6 * rows * width, transcendentals=0
        ),
        name="disarrange",
    )(spot, own, other)


ALL = ("dp", "ctx")


def hop(value, way):
    ways = lax.axis_size("ctx")
    return lax.ppermute(value, "ctx", [(c, c ^ way) for c in range(ways)])


def gather_near(value):
    ways = lax.axis_size("ctx")
    return [value] + [hop(value, way) for way in range(1, 3 if ways == 4 else ways)]


def gather_far(parts):
    if lax.axis_size("ctx") != 4:
        return parts
    half = parts[0].shape[0] // 2
    far = [hop(parts[1][:half], 2), hop(parts[2][half:], 1)]
    return parts + far


def gather_rows(value):
    return jnp.concatenate(gather_far(gather_near(value)), axis=0)


def scatter_rows(far, near):
    ways = lax.axis_size("ctx")
    size = far.shape[0]
    near = [near[way * size : (way + 1) * size] for way in range(ways - 1)]
    far = far.astype(bf16)
    if ways != 4:
        total = near[0]
        for way, part in enumerate(near[1:] + [far], 1):
            total = total + hop(part.astype(bf16), way).astype(f32)
        return total
    half = size // 2
    upper, lower = hop(far[:half], 1), hop(far[half:], 2)
    nothing = jnp.zeros_like(upper)
    one = near[1] + jnp.concatenate([nothing, lower], axis=0).astype(f32)
    two = near[2] + jnp.concatenate([upper, nothing], axis=0).astype(f32)
    one, two = hop(one.astype(bf16), 1), hop(two.astype(bf16), 2)
    return near[0] + one.astype(f32) + two.astype(f32)


def exchange(pieces):
    return [pieces[0]] + [hop(piece, way) for way, piece in enumerate(pieces) if way]


def place_parts(parts, axis):
    me = lax.axis_index("ctx")
    return jnp.concatenate(
        [lax.select_n(me ^ place, *parts) for place in range(len(parts))], axis=axis
    )


def doubling(value, axis, bits):
    size, me = lax.axis_size(axis), lax.axis_index(axis)
    for bit in bits:
        other = lax.ppermute(value, axis, [(d, d ^ bit) for d in range(size)])
        upper = (me & bit) != 0
        value = jnp.where(
            upper,
            jnp.concatenate([other, value], axis=0),
            jnp.concatenate([value, other], axis=0),
        )
    return value


def halving(value, axis, bits):
    size, me = lax.axis_size(axis), lax.axis_index(axis)
    for bit in bits:
        half = value.shape[0] // 2
        upper = (me & bit) != 0
        keep = jnp.where(upper, value[half:], value[:half])
        give = jnp.where(upper, value[:half], value[half:])
        value = keep + lax.ppermute(give, axis, [(d, d ^ bit) for d in range(size)])
    return value


def bits_of(size):
    return [1 << n for n in range(size.bit_length() - 1)]


def core_swap(value):
    groups = lax.axis_size("dp")
    return lax.ppermute(value, "dp", [(d, d ^ 1) for d in range(groups)])


def shards(
    residual_in,
    document_ids,
    attention_gain,
    attention_shift,
    query_key_value,
    query_value_bias,
    output_weight,
    output_bias,
    feedforward_gain,
    feedforward_shift,
    expand_weight,
    expand_bias,
    contract_weight,
    contract_bias,
    output_grad,
):
    groups, ways = lax.axis_size("dp"), lax.axis_size("ctx")
    me_dp, me = lax.axis_index("dp"), lax.axis_index("ctx")
    seqs, stretch, width = residual_in.shape
    assert seqs == 1
    length = stretch * ways
    slab = query_key_value.shape[0]
    inner_slab = contract_weight.shape[0]
    features = width // ways
    heads = HEADS // ways
    line, core, spot = groups // 2, me_dp & 1, me_dp >> 1

    def rows_of(value, way):
        return value[way * stretch : (way + 1) * stretch]

    def pieces_of(value, count):
        size = value.shape[1] // (count * ways)
        absolute = [
            jnp.concatenate(
                [value[:, (n * ways + p) * size : (n * ways + p + 1) * size] for n in range(count)], 1
            )
            for p in range(ways)
        ]
        return [lax.select_n(me ^ way, *absolute) for way in range(ways)]

    def gather_dp(value):
        return lax.all_gather(value, "dp", axis=0, tiled=True)

    def core_columns(value, core):
        size = value.shape[1] // groups
        return jnp.concatenate(
            [lax.dynamic_slice_in_dim(value, (2 * n + core) * size, size, 1) for n in range(line)], 1
        )

    def core_term(left, right):
        give = dot(core_columns(left, core ^ 1), right, ((0,), (0,))).astype(bf16)
        keep = dot(core_columns(left, core), right, ((0,), (0,)))
        return (keep + core_swap(give).astype(f32)).astype(bf16)

    def scatter_dp(value):
        return lax.psum_scatter(value, "dp", scatter_dimension=0, tiled=True)

    def scatter_line(value):
        lines = [[2 * n + core for n in range(line)] for core in range(2)]
        return lax.psum_scatter(
            value, "dp", scatter_dimension=0, tiled=True, axis_index_groups=lines
        )

    def split_rows(left, right, contract):
        last = (ways - 1) * stretch
        return dot(left[last:], right, contract), dot(left[:last], right, contract)

    def own_rows(grad, count):
        pieces = [
            lax.dynamic_slice_in_dim(grad, (me ^ way) * slab, slab, 0) for way in range(ways)
        ]
        parts = exchange(pieces)
        parts = [lax.select_n(me ^ place, *parts) for place in range(ways)]
        size = grad.shape[1] // count
        return jnp.concatenate(
            [part[:, n * size : (n + 1) * size] for n in range(count) for part in parts], axis=1
        ).astype(f32)

    small = (
        attention_gain,
        attention_shift,
        output_bias,
        feedforward_gain,
        feedforward_shift,
        contract_bias,
        query_value_bias,
        expand_bias,
    )
    every = range(ways)
    packed = jnp.concatenate(small)[None]
    qkv_parts = exchange(pieces_of(query_key_value, 3))
    out_parts = [output_weight] + [
        lax.ppermute(output_weight, "dp", [(d, (d + 2 * n) % groups) for d in range(groups)])
        for n in range(1, line)
    ]
    block = residual_in[0]
    docs_all = jnp.concatenate([hop(document_ids[0], way) if way else document_ids[0] for way in every])
    packed = place_parts(
        [hop(packed, way) if way else packed for way in every], 0
    )
    qkv_parts, out_parts, docs_all, expand_weight, block, packed = lax.optimization_barrier(
        (qkv_parts, out_parts, docs_all, expand_weight, block, packed)
    )
    qkv_weight = gather_dp(place_parts(qkv_parts, 0))
    exp_parts = exchange(pieces_of(expand_weight, groups))
    packed = doubling(packed, "dp", bits_of(groups))
    block_near = gather_near(block)
    block_near, packed = lax.optimization_barrier((block_near, packed))
    block_all = jnp.concatenate(gather_far(block_near), axis=0)
    out_mine = jnp.concatenate(
        [lax.select_n((spot - n + line) % line, *out_parts) for n in range(line)], axis=0
    )
    block_all, exp_parts, out_mine = lax.optimization_barrier((block_all, exp_parts, out_mine))
    packed = packed.astype(f32)
    whole, at = [], 0
    for item in small:
        whole.append(packed[:, at : at + item.shape[0]].reshape(-1))
        at += item.shape[0]
    att_gain, att_shift, out_bias, ff_gain, ff_shift, con_bias, qv_bias, exp_bias = whole
    exp_bias = lax.dynamic_index_in_dim(
        exp_bias.reshape(groups, ways, inner_slab), me, 1, keepdims=False
    ).reshape(-1)
    qv_bias = lax.dynamic_index_in_dim(qv_bias.reshape(2, ways, features), me, 1, keepdims=False)
    exp_weight = gather_dp(place_parts(exp_parts, 0))
    con_weight = gather_dp(contract_weight)
    out_near = gather_near(out_mine)
    grad_out = output_grad[0]
    starts = (docs_all - me_dp * length)[:, None]
    slopes = jnp.exp2(
        -8.0 * ((me * heads + jnp.arange(heads, dtype=jnp.int32)).astype(f32) + 1.0) / HEADS
    )

    rows = block.astype(f32)
    unit_in, scale_in = unit_rows(rows)
    normed_low = (unit_rows(block_all.astype(f32))[0] * att_gain + att_shift).astype(bf16)
    bias = jnp.concatenate([qv_bias[0], jnp.zeros((features,), f32), qv_bias[1]])
    projected = (dot(normed_low, qkv_weight) + bias).astype(bf16)
    projected, out_near = lax.optimization_barrier((projected, out_near))
    out_own = [item.reshape(-1, slab, width) for item in gather_far(out_near)]
    if ways == 4:
        out_own[3:] = [jnp.concatenate(out_own[3:], axis=0)]
    out_own = jnp.stack(out_own, axis=1).reshape(width // 2, width)
    out_other = core_swap(out_own)
    grad_near = gather_near(grad_out)
    me_array = me.reshape(1)
    attended, probs = attend_forward(stretch, me_array, slopes, starts, projected)
    attended, grad_near = lax.optimization_barrier((attended, grad_near))
    device = jnp.stack([me, core])
    rows_own, rows_other = arrange(
        slab, device, exchange([rows_of(attended, way) for way in every])
    )
    middle = rows + dot(rows_own, out_own) + dot(rows_other, out_other) + out_bias

    unit_mid, scale_mid = unit_rows(middle)
    normed_mid = gather_rows((unit_mid * ff_gain + ff_shift).astype(bf16))
    normed_mid, grad_near[1] = lax.optimization_barrier((normed_mid, grad_near[1]))
    grad_out_all = jnp.concatenate(gather_far(grad_near), axis=0)
    inner = dot(normed_mid, exp_weight) + exp_bias
    cumulative = (1.0 + lax.erf(inner * 0.7071067811865476)) * 0.5
    active = (inner * cumulative).astype(bf16)
    con_term = dot(active, grad_out_all, ((0,), (0,))).astype(bf16)
    con_term, con_weight = lax.optimization_barrier((con_term, con_weight))
    con_sum = scatter_dp(con_term)
    grad_active = dot(grad_out_all, con_weight, ((1,), (1,)))
    density = jnp.exp(-0.5 * inner * inner) * 0.3989422804014327
    grad_inner = (grad_active * (cumulative + inner * density)).astype(bf16)
    far, near = split_rows(grad_inner, exp_weight, ((1,), (1,)))
    exp_term = dot(normed_mid, grad_inner, ((0,), (0,))).astype(bf16)
    exp_bias_term = jnp.sum(grad_inner.astype(f32), axis=0)
    grad_normed_mid = scatter_rows(far, near)
    exp_term, grad_normed_mid = lax.optimization_barrier((exp_term, grad_normed_mid))
    exp_sum = scatter_dp(exp_term)
    grad_mid_norm, ff_gain_term, ff_shift_term = norm_backward(
        grad_normed_mid, unit_mid, scale_mid, ff_gain
    )
    grad_out_full = grad_out.astype(f32)
    grad_middle = grad_out_full + grad_mid_norm
    grad_branch = grad_middle.astype(bf16)

    grad_heads = disarrange(
        slab,
        device,
        dot(grad_branch, out_own, ((1,), (1,))),
        dot(grad_branch, out_other, ((1,), (1,))),
        ways,
    )
    grad_heads = jnp.concatenate(exchange(grad_heads), axis=0)
    grad_heads, active = lax.optimization_barrier((grad_heads, active))
    result = dot(active, con_weight)
    result = scatter_rows(result[(ways - 1) * stretch :], result)
    layer_output = (middle + result + con_bias).astype(bf16)[None]
    grad_projected = jnp.concatenate(
        attend_backward(stretch, me_array, probs, projected, grad_heads), axis=1
    )
    qkv_term = dot(normed_low, grad_projected, ((0,), (0,))).astype(bf16)
    qkv_term, con_sum = lax.optimization_barrier((qkv_term, con_sum))
    give = dot(rows_other, grad_branch, ((0,), (0,))).astype(bf16)
    out_term = dot(rows_own, grad_branch, ((0,), (0,))) + core_swap(give).astype(f32)
    out_term = out_term.reshape(line, ways, slab, width)
    out_term = [out_term[:, way].reshape(line * slab, width) for way in every]
    out_term = scatter_rows(out_term[-1], jnp.concatenate(out_term[:-1], axis=0)).astype(bf16)
    qkv_term, grad_projected, exp_sum, layer_output, out_term = lax.optimization_barrier(
        (qkv_term, grad_projected, exp_sum, layer_output, out_term)
    )
    far, near = split_rows(grad_projected, qkv_weight, ((1,), (1,)))
    grad_normed_in = scatter_rows(far, near)
    exp_grad = own_rows(exp_sum, groups)
    qkv_sum = scatter_dp(qkv_term)
    grad_in_norm, att_gain_term, att_shift_term = norm_backward(
        grad_normed_in, unit_in, scale_in, att_gain
    )
    input_grad = (grad_middle + grad_in_norm).astype(bf16)[None]

    bias_sums = jnp.sum(grad_projected.astype(f32), axis=0).reshape(3, features)
    qv_term = lax.dynamic_update_slice(
        jnp.zeros((2, ways, features), f32),
        jnp.stack([bias_sums[0], bias_sums[2]])[:, None],
        (0, me, 0),
    ).reshape(-1)
    exp_term = lax.dynamic_update_slice(
        jnp.zeros((groups, ways, inner_slab), f32),
        exp_bias_term.reshape(groups, 1, inner_slab),
        (0, me, 0),
    ).reshape(-1)
    terms = (
        att_gain_term,
        att_shift_term,
        jnp.sum(grad_branch.astype(f32), axis=0),
        ff_gain_term,
        ff_shift_term,
        jnp.sum(grad_out_full, axis=0),
        qv_term,
        exp_term,
    )
    count = groups * ways
    sums = jnp.concatenate([item.reshape(count, -1) for item in terms], axis=1)
    out_grad = halving(out_term.reshape(line, slab, width), "dp", bits_of(groups)[:0:-1])
    out_grad = out_grad[0].astype(f32)
    sums = halving(sums, "dp", bits_of(groups)[::-1])
    sums = halving(sums, "ctx", bits_of(ways)[::-1]).reshape(-1)
    sums, qkv_sum, out_grad, exp_grad = lax.optimization_barrier(
        (sums, qkv_sum, out_grad, exp_grad)
    )
    qkv_grad = own_rows(qkv_sum, 3)
    own, at = [], 0
    for item in small:
        own.append(sums[at : at + item.shape[0]])
        at += item.shape[0]
    return (
        layer_output,
        input_grad,
        own[0],
        own[1],
        qkv_grad,
        own[6],
        out_grad,
        own[2],
        own[3],
        own[4],
        exp_grad,
        own[7],
        con_sum.astype(f32),
        own[5],
    )


def solution(mesh):
    tokens = P("dp", "ctx", None)
    vector = P(ALL)
    matrix = P(ALL, None)
    in_specs = (
        tokens,
        P("dp", "ctx"),
        vector,
        vector,
        matrix,
        vector,
        matrix,
        vector,
        vector,
        vector,
        matrix,
        vector,
        matrix,
        vector,
        tokens,
    )
    out_specs = (
        tokens,
        tokens,
        vector,
        vector,
        matrix,
        vector,
        matrix,
        vector,
        vector,
        vector,
        matrix,
        vector,
        matrix,
        vector,
    )
    return jax.shard_map(shards, mesh=mesh, in_specs=in_specs, out_specs=out_specs, check_vma=False)
```

```python
import functools

import jax
import jax.numpy as jnp
from jax import lax
from jax.experimental import pallas as pl
from jax.experimental.pallas import tpu as pltpu
from jax.sharding import PartitionSpec as P

HEADS = 32
HEAD_DIM = 64
PAIR = 2 * HEAD_DIM

bf16 = jnp.bfloat16
f32 = jnp.float32
epsilon = 1e-05


def unit_rows(value):
    mean = jnp.mean(value, axis=-1, keepdims=True)
    centred = value - mean
    scale = lax.rsqrt(jnp.mean(centred * centred, axis=-1, keepdims=True) + epsilon)
    return centred * scale, scale


def norm_backward(grad, unit, scale, gain):
    scaled = grad * gain
    level = jnp.mean(scaled, axis=-1, keepdims=True)
    along = jnp.mean(scaled * unit, axis=-1, keepdims=True)
    return (
        scale * (scaled - level - unit * along),
        jnp.sum(grad * unit, axis=0),
        jnp.sum(grad, axis=0),
    )


def dot(left, right, contract=((1,), (0,))):
    return lax.dot_general(left, right, (contract, ((), ())), preferred_element_type=f32)


def lane_mask(half):
    lane = lax.broadcasted_iota(jnp.int32, (1, PAIR), 1)
    return (lane >= HEAD_DIM) if half else (lane < HEAD_DIM)


def stretch_rows(me_ref, index, block):
    return pl.ds(pl.multiple_of((index ^ me_ref[0]) * block, block), block)


def in_order(me_ref, source, target, block):
    for index in range(source.shape[0] // block):
        target[pl.ds(index * block, block), :] = source[stretch_rows(me_ref, index, block), :]


def attend_forward_kernel(
    block, me_ref, slope_ref, start_ref, q_ref, k_in, v_in, out_ref, probs_ref, k_ref, v_ref
):
    length = q_ref.shape[0]
    pair = pl.program_id(0)
    in_order(me_ref, k_in, k_ref, block)
    in_order(me_ref, v_in, v_ref, block)
    for index in range(length // block):
        rows = stretch_rows(me_ref, index, block)
        place = pl.ds(index * block, block)
        span = (index + 1) * block
        starts = start_ref[rows, :]
        q_place = index * block + lax.broadcasted_iota(jnp.int32, (block, span), 0)
        k_place = lax.broadcasted_iota(jnp.int32, (block, span), 1)
        visible = (k_place >= starts) & (k_place <= q_place)
        k_row = lax.broadcasted_iota(jnp.int32, (1, span), 1).astype(f32)
        mixed = []
        for half in range(2):
            slope = slope_ref[pair * 2 + half]
            query = jnp.where(lane_mask(half), q_ref[rows, :] * bf16(0.125), bf16(0))
            scores = dot(query, k_ref[:span, :], ((1,), (1,))) + slope * k_row
            scores = jnp.where(visible, scores, -1e30)
            top = jnp.max(scores, axis=-1, keepdims=True)
            weights = jnp.exp(scores - top)
            total = jnp.sum(weights, axis=-1, keepdims=True)
            probs = (weights * (1.0 / total)).astype(bf16)
            probs_ref[half, place, :span] = probs
            mixed.append(dot(probs, v_ref[:span, :]))
        out_ref[rows, :] = jnp.where(lane_mask(0), mixed[0], mixed[1]).astype(bf16)


def attend_backward_kernel(
    block, me_ref, probs_ref, q_ref, k_in, v_in, g_ref, dq_ref, dk_ref, dv_ref, k_ref, v_ref, dk_sum, dv_sum
):
    length = q_ref.shape[0]
    in_order(me_ref, k_in, k_ref, block)
    in_order(me_ref, v_in, v_ref, block)
    dk_sum[...] = jnp.zeros_like(dk_sum)
    dv_sum[...] = jnp.zeros_like(dv_sum)
    for index in range(length // block):
        rows = stretch_rows(me_ref, index, block)
        place = pl.ds(index * block, block)
        span = (index + 1) * block
        parts = []
        for half in range(2):
            mask = lane_mask(half)
            grad = jnp.where(mask, g_ref[rows, :], bf16(0))
            query = jnp.where(mask, q_ref[rows, :] * bf16(0.125), bf16(0))
            probs_low = probs_ref[half, place, :span]
            probs = probs_low.astype(f32)
            grad_probs = dot(grad, v_ref[:span, :], ((1,), (1,)))
            along = jnp.sum(probs * grad_probs, axis=-1, keepdims=True)
            grad_scores = (probs * (grad_probs - along)).astype(bf16)
            parts.append(dot(grad_scores, k_ref[:span, :]))
            dk_sum[:span, :] += dot(grad_scores, query, ((0,), (0,)))
            dv_sum[:span, :] += dot(probs_low, grad, ((0,), (0,)))
        dq_ref[rows, :] = (jnp.where(lane_mask(0), parts[0], parts[1]) * 0.125).astype(bf16)
    for index in range(length // block):
        rows = stretch_rows(me_ref, index, block)
        place = pl.ds(index * block, block)
        dk_ref[rows, :] = dk_sum[place, :].astype(bf16)
        dv_ref[rows, :] = dv_sum[place, :].astype(bf16)


def attend_forward(block, me, slopes, starts, projected):
    length = projected.shape[0]
    heads = projected.shape[1] // (3 * HEAD_DIM)
    pairs = heads // 2
    column = lambda first: pl.BlockSpec((length, PAIR), lambda p: (0, first + p))
    return pl.pallas_call(
        functools.partial(attend_forward_kernel, block),
        grid=(pairs,),
        in_specs=[
            pl.BlockSpec(memory_space=pltpu.SMEM),
            pl.BlockSpec(memory_space=pltpu.SMEM),
            pl.BlockSpec((length, 1), lambda p: (0, 0)),
            column(0),
            column(pairs),
            column(2 * pairs),
        ],
        out_specs=[column(0), pl.BlockSpec((2, length, length), lambda p: (p, 0, 0))],
        out_shape=[
            jax.ShapeDtypeStruct((length, heads * HEAD_DIM), bf16),
            jax.ShapeDtypeStruct((heads, length, length), bf16),
        ],
        scratch_shapes=[pltpu.VMEM((length, PAIR), bf16), pltpu.VMEM((length, PAIR), bf16)],
        compiler_params=pltpu.CompilerParams(vmem_limit_bytes=50 * 2**20),
        cost_estimate=pl.CostEstimate(
            flops=4 * heads * length * length * PAIR,
            bytes_accessed=2 * heads * length * length,
            transcendentals=heads * length * length,
        ),
        name="attend_forward",
    )(me, slopes, starts, projected, projected, projected)


def attend_backward(block, me, probs, projected, grad):
    length = projected.shape[0]
    heads = projected.shape[1] // (3 * HEAD_DIM)
    pairs = heads // 2
    column = lambda first: pl.BlockSpec((length, PAIR), lambda p: (0, first + p))
    shape = jax.ShapeDtypeStruct((length, heads * HEAD_DIM), bf16)
    return pl.pallas_call(
        functools.partial(attend_backward_kernel, block),
        grid=(pairs,),
        in_specs=[
            pl.BlockSpec(memory_space=pltpu.SMEM),
            pl.BlockSpec((2, length, length), lambda p: (p, 0, 0)),
            column(0),
            column(pairs),
            column(2 * pairs),
            column(0),
        ],
        out_specs=[column(0), column(0), column(0)],
        out_shape=[shape, shape, shape],
        scratch_shapes=[
            pltpu.VMEM((length, PAIR), bf16),
            pltpu.VMEM((length, PAIR), bf16),
            pltpu.VMEM((length, PAIR), f32),
            pltpu.VMEM((length, PAIR), f32),
        ],
        compiler_params=pltpu.CompilerParams(vmem_limit_bytes=50 * 2**20),
        cost_estimate=pl.CostEstimate(
            flops=8 * heads * length * length * PAIR,
            bytes_accessed=2 * heads * length * length,
            transcendentals=0,
        ),
        name="attend_backward",
    )(me, probs, projected, projected, projected, grad)


def relative_slabs(value, me, ways, slab):
    width = value.shape[1]
    lane = lax.broadcasted_iota(jnp.int32, (1, width), 1)
    bit = 1
    while bit < ways:
        size = bit * slab
        upper, lower = pltpu.roll(value, size, 1), pltpu.roll(value, width - size, 1)
        swapped = jnp.where((lane & size) != 0, upper, lower)
        value = jnp.where((me & bit) != 0, swapped, value)
        bit *= 2
    return value


def arrange_kernel(slab, spot_ref, *refs):
    *part_refs, own_ref, other_ref, whole = refs
    ways = len(part_refs)
    me, core = spot_ref[0], spot_ref[1]
    features, width = part_refs[0].shape[1], whole.shape[1]
    for way, ref in enumerate(part_refs):
        place = pl.ds(pl.multiple_of((me ^ way) * features, 128), features)
        whole[:, place] = ref[...].astype(f32)
    whole[...] = relative_slabs(whole[...], me, ways, slab)
    size = ways * slab
    for n in range(width // (2 * size)):
        for which, ref in ((0, own_ref), (1, other_ref)):
            place = pl.ds(pl.multiple_of((2 * n + (core ^ which)) * size, 128), size)
            ref[:, n * size : (n + 1) * size] = whole[:, place].astype(bf16)


def disarrange_kernel(slab, spot_ref, own_ref, other_ref, *refs):
    *part_refs, whole = refs
    ways = len(part_refs)
    me, core = spot_ref[0], spot_ref[1]
    features, width = part_refs[0].shape[1], whole.shape[1]
    size = ways * slab
    for n in range(width // (2 * size)):
        for which, ref in ((0, own_ref), (1, other_ref)):
            place = pl.ds(pl.multiple_of((2 * n + (core ^ which)) * size, 128), size)
            whole[:, place] = ref[:, n * size : (n + 1) * size]
    whole[...] = relative_slabs(whole[...], me, ways, slab)
    for way, ref in enumerate(part_refs):
        place = pl.ds(pl.multiple_of((me ^ way) * features, 128), features)
        ref[...] = whole[:, place].astype(bf16)


def arrange(slab, spot, parts):
    rows, features = parts[0].shape
    width = features * len(parts)
    vmem = pl.BlockSpec(memory_space=pltpu.VMEM)
    half = jax.ShapeDtypeStruct((rows, width // 2), bf16)
    return pl.pallas_call(
        functools.partial(arrange_kernel, slab),
        in_specs=[pl.BlockSpec(memory_space=pltpu.SMEM)] + [vmem] * len(parts),
        out_specs=[vmem, vmem],
        out_shape=[half, half],
        scratch_shapes=[pltpu.VMEM((rows, width), f32)],
        compiler_params=pltpu.CompilerParams(vmem_limit_bytes=32 * 2**20),
        cost_estimate=pl.CostEstimate(
            flops=16 * rows * width, bytes_accessed=4 * rows * width, transcendentals=0
        ),
        name="arrange",
    )(spot, *parts)


def disarrange(slab, spot, own, other, ways):
    rows, width = own.shape[0], 2 * own.shape[1]
    vmem = pl.BlockSpec(memory_space=pltpu.VMEM)
    part = jax.ShapeDtypeStruct((rows, width // ways), bf16)
    return pl.pallas_call(
        functools.partial(disarrange_kernel, slab),
        in_specs=[pl.BlockSpec(memory_space=pltpu.SMEM), vmem, vmem],
        out_specs=[vmem] * ways,
        out_shape=[part] * ways,
        scratch_shapes=[pltpu.VMEM((rows, width), f32)],
        compiler_params=pltpu.CompilerParams(vmem_limit_bytes=32 * 2**20),
        cost_estimate=pl.CostEstimate(
            flops=16 * rows * width, bytes_accessed=6 * rows * width, transcendentals=0
        ),
        name="disarrange",
    )(spot, own, other)


def lay_kernel(count, spot_ref, *refs):
    *part_refs, out_ref = refs
    ways = len(part_refs)
    size = part_refs[0].shape[1] // count
    for way, ref in enumerate(part_refs):
        for n in range(count):
            place = pl.multiple_of((n * ways + (way ^ spot_ref[0])) * size, 128)
            out_ref[:, pl.ds(place, size)] = ref[:, n * size : (n + 1) * size].astype(f32)


def lay(count, spot, parts):
    rows, width = parts[0].shape[0], parts[0].shape[1] * len(parts)
    vmem = pl.BlockSpec(memory_space=pltpu.VMEM)
    return pl.pallas_call(
        functools.partial(lay_kernel, count),
        in_specs=[pl.BlockSpec(memory_space=pltpu.SMEM)] + [vmem] * len(parts),
        out_specs=vmem,
        out_shape=jax.ShapeDtypeStruct((rows, width), f32),
        compiler_params=pltpu.CompilerParams(vmem_limit_bytes=32 * 2**20),
        cost_estimate=pl.CostEstimate(
            flops=0, bytes_accessed=6 * rows * width, transcendentals=0
        ),
        name="lay",
    )(spot, *parts)


def pack_kernel(*refs):
    *item_refs, out_ref = refs
    width = out_ref.shape[1]
    rows = []
    for ref in item_refs:
        row, rest = ref[...].astype(f32), width - ref.shape[1]
        rows.append(jnp.concatenate([row, jnp.zeros((1, rest), f32)], axis=1) if rest else row)
    rest = out_ref.shape[0] - len(rows)
    rows.append(jnp.zeros((rest, width), f32))
    out_ref[...] = jnp.concatenate(rows, axis=0).astype(bf16)


def pack(items, width):
    vmem = pl.BlockSpec(memory_space=pltpu.VMEM)
    return pl.pallas_call(
        pack_kernel,
        in_specs=[vmem] * len(items),
        out_specs=vmem,
        out_shape=jax.ShapeDtypeStruct((16, width), bf16),
        name="pack",
    )(*[item[None] for item in items])


ALL = ("dp", "ctx")


def hop(value, way):
    ways = lax.axis_size("ctx")
    return lax.ppermute(value, "ctx", [(c, c ^ way) for c in range(ways)])


def gather_near(value):
    ways, half = lax.axis_size("ctx"), value.shape[0] // 2
    halves = [value[:half], value[half:]]
    return [halves] + [
        [hop(item, way) for item in halves] for way in range(1, 3 if ways == 4 else ways)
    ]


def gather_far(parts):
    if lax.axis_size("ctx") == 4:
        parts = parts + [[hop(parts[1][0], 2), hop(parts[2][1], 1)]]
    return [item for halves in parts for item in halves]


def gather_rows(value):
    return jnp.concatenate(gather_far(gather_near(value)), axis=0)


def halves_of(near, ways):
    half = near.shape[0] // (2 * ways - 2)
    return [near[n * half : (n + 1) * half] for n in range(2 * ways - 2)]


def scatter_far(far):
    far, half = far.astype(bf16), far.shape[0] // 2
    if lax.axis_size("ctx") != 4:
        return [far[:half], far[half:]]
    return [hop(far[:half], 1), hop(far[half:], 2)]


def scatter_side(near):
    ways = lax.axis_size("ctx")
    near = halves_of(near, ways)
    if ways != 4:
        return [item.astype(bf16) for item in near[2:4]]
    return [hop(near[2].astype(bf16), 1), hop(near[5].astype(bf16), 2)]


def scatter_near(near, far, side):
    ways = lax.axis_size("ctx")
    near = halves_of(near, ways)
    total = near[:2]
    if ways != 4:
        for n, part in enumerate(side + near[4:] + far):
            total[n % 2] = total[n % 2] + hop(part.astype(bf16), 1 + n // 2).astype(f32)
    else:
        upper, lower = far
        one = hop((near[3] + lower.astype(f32)).astype(bf16), 1)
        two = hop((near[4] + upper.astype(f32)).astype(bf16), 2)
        total[0] = total[0] + side[0].astype(f32) + two.astype(f32)
        total[1] = total[1] + side[1].astype(f32) + one.astype(f32)
    return jnp.concatenate(total, axis=0)


def scatter_rows(far, near):
    return scatter_near(near, scatter_far(far), scatter_side(near))


def exchange(pieces):
    return [pieces[0]] + [hop(piece, way) for way, piece in enumerate(pieces) if way]


def place_parts(parts, axis):
    me = lax.axis_index("ctx")
    return jnp.concatenate(
        [lax.select_n(me ^ place, *parts) for place in range(len(parts))], axis=axis
    )


def doubling(value, axis, bits):
    size, me = lax.axis_size(axis), lax.axis_index(axis)
    for bit in bits:
        other = lax.ppermute(value, axis, [(d, d ^ bit) for d in range(size)])
        upper = (me & bit) != 0
        value = jnp.where(
            upper,
            jnp.concatenate([other, value], axis=0),
            jnp.concatenate([value, other], axis=0),
        )
    return value


def halving(value, axis, bits):
    size, me = lax.axis_size(axis), lax.axis_index(axis)
    for bit in bits:
        half = value.shape[0] // 2
        upper = (me & bit) != 0
        keep = jnp.where(upper, value[half:], value[:half])
        give = jnp.where(upper, value[:half], value[half:])
        value = keep + lax.ppermute(give, axis, [(d, d ^ bit) for d in range(size)])
    return value


def bits_of(size):
    return [1 << n for n in range(size.bit_length() - 1)]


def core_swap(value):
    groups = lax.axis_size("dp")
    return lax.ppermute(value, "dp", [(d, d ^ 1) for d in range(groups)])


def shards(
    residual_in,
    document_ids,
    attention_gain,
    attention_shift,
    query_key_value,
    query_value_bias,
    output_weight,
    output_bias,
    feedforward_gain,
    feedforward_shift,
    expand_weight,
    expand_bias,
    contract_weight,
    contract_bias,
    output_grad,
):
    groups, ways = lax.axis_size("dp"), lax.axis_size("ctx")
    me_dp, me = lax.axis_index("dp"), lax.axis_index("ctx")
    seqs, stretch, width = residual_in.shape
    assert seqs == 1
    length = stretch * ways
    slab = query_key_value.shape[0]
    inner_slab = contract_weight.shape[0]
    features = width // ways
    heads = HEADS // ways
    line, core, spot = groups // 2, me_dp & 1, me_dp >> 1

    def rows_of(value, way):
        return value[way * stretch : (way + 1) * stretch]

    def pieces_of(value, count):
        size = value.shape[1] // (count * ways)
        absolute = [
            jnp.concatenate(
                [value[:, (n * ways + p) * size : (n * ways + p + 1) * size] for n in range(count)], 1
            )
            for p in range(ways)
        ]
        return [lax.select_n(me ^ way, *absolute) for way in range(ways)]

    def gather_dp(value):
        return lax.all_gather(value, "dp", axis=0, tiled=True)

    def core_columns(value, core):
        size = value.shape[1] // groups
        return jnp.concatenate(
            [lax.dynamic_slice_in_dim(value, (2 * n + core) * size, size, 1) for n in range(line)], 1
        )

    def core_term(left, right):
        give = dot(core_columns(left, core ^ 1), right, ((0,), (0,))).astype(bf16)
        keep = dot(core_columns(left, core), right, ((0,), (0,)))
        return (keep + core_swap(give).astype(f32)).astype(bf16)

    def scatter_dp(value):
        return lax.psum_scatter(value, "dp", scatter_dimension=0, tiled=True)

    def scatter_line(value):
        lines = [[2 * n + core for n in range(line)] for core in range(2)]
        return lax.psum_scatter(
            value, "dp", scatter_dimension=0, tiled=True, axis_index_groups=lines
        )

    def split_rows(left, right, contract):
        last = (ways - 1) * stretch
        return dot(left[last:], right, contract), dot(left[:last], right, contract)

    def own_rows(grad, count):
        pieces = [
            lax.dynamic_slice_in_dim(grad, (me ^ way) * slab, slab, 0) for way in range(ways)
        ]
        parts = exchange(pieces)
        size = grad.shape[1] // count
        if size % 128 == 0:
            return lay(count, me.reshape(1), parts)
        parts = [lax.select_n(me ^ place, *parts) for place in range(ways)]
        return jnp.concatenate(
            [part[:, n * size : (n + 1) * size] for n in range(count) for part in parts], axis=1
        ).astype(f32)

    small = (
        attention_gain,
        attention_shift,
        output_bias,
        feedforward_gain,
        feedforward_shift,
        contract_bias,
        query_value_bias,
        expand_bias,
    )
    every = range(ways)
    begin = (document_ids[0] - me_dp * length).reshape(-1, inner_slab)
    kinds, lines = len(small), begin.shape[0]
    begin = [*(begin >> 5).astype(bf16), *(begin & 31).astype(bf16)]
    qkv_parts = exchange(pieces_of(query_key_value, 3))
    out_block = jnp.concatenate([output_weight, pack([*small, *begin], width)], axis=0)
    out_parts = [out_block] + [
        lax.ppermute(out_block, "dp", [(d, (d + 2 * n) % groups) for d in range(groups)])
        for n in range(1, line)
    ]
    block = residual_in[0]
    qkv_parts, out_parts, expand_weight, block = lax.optimization_barrier(
        (qkv_parts, out_parts, expand_weight, block)
    )
    qkv_weight = gather_dp(place_parts(qkv_parts, 0))
    packs = [part[slab:, :inner_slab] for part in out_parts]
    packs = [lax.select_n((spot - n + line) % line, *packs) for n in range(line)]
    other = core_swap(jnp.concatenate(packs, axis=1))
    packed = []
    for n, mine in enumerate(packs):
        theirs = other[:, n * inner_slab : (n + 1) * inner_slab]
        packed += [jnp.where(core == 0, mine, theirs), jnp.where(core == 0, theirs, mine)]
    packed = jnp.concatenate(packed, axis=1)
    exp_parts = exchange(
        [jnp.concatenate([piece, packed], axis=0) for piece in pieces_of(expand_weight, groups)]
    )
    block_all = gather_rows(block)
    out_mine = jnp.concatenate(
        [
            lax.select_n((spot - n + line) % line, *[part[:slab] for part in out_parts])
            for n in range(line)
        ],
        axis=0,
    )
    block_all, exp_parts, out_mine = lax.optimization_barrier((block_all, exp_parts, out_mine))
    packs = [part[slab:] for part in exp_parts]
    exp_parts = [part[:slab] for part in exp_parts]
    begin = [
        lax.dynamic_slice_in_dim(part[kinds : kinds + 2 * lines], me_dp * inner_slab, inner_slab, 1)
        for part in packs
    ]
    begin = [32.0 * item[:lines].astype(f32) + item[lines:].astype(f32) for item in begin]
    starts = jnp.concatenate(begin, axis=0).astype(jnp.int32).reshape(length, 1)
    packed = [part[:kinds].astype(f32).reshape(kinds, groups, inner_slab) for part in packs]
    packed = jnp.stack([lax.select_n(me ^ place, *packed) for place in every], axis=2)
    whole = [packed[n, :, :, : item.shape[0]].reshape(-1) for n, item in enumerate(small)]
    att_gain, att_shift, out_bias, ff_gain, ff_shift, con_bias, qv_bias, exp_bias = whole
    exp_bias = lax.dynamic_index_in_dim(
        exp_bias.reshape(groups, ways, inner_slab), me, 1, keepdims=False
    ).reshape(-1)
    qv_bias = lax.dynamic_index_in_dim(qv_bias.reshape(2, ways, features), me, 1, keepdims=False)
    exp_weight = gather_dp(place_parts(exp_parts, 0))
    con_weight = gather_dp(contract_weight)
    out_near = gather_near(out_mine)
    grad_out = output_grad[0]
    slopes = jnp.exp2(
        -8.0 * ((me * heads + jnp.arange(heads, dtype=jnp.int32)).astype(f32) + 1.0) / HEADS
    )

    rows = block.astype(f32)
    unit_in, scale_in = unit_rows(rows)
    normed_low = (unit_rows(block_all.astype(f32))[0] * att_gain + att_shift).astype(bf16)
    bias = jnp.concatenate([qv_bias[0], jnp.zeros((features,), f32), qv_bias[1]])
    projected = (dot(normed_low, qkv_weight) + bias).astype(bf16)
    projected, out_near = lax.optimization_barrier((projected, out_near))
    out_all = gather_far(out_near)
    grad_near = gather_near(grad_out)
    me_array = me.reshape(1)
    attended, probs = attend_forward(stretch, me_array, slopes, starts, projected)
    attended, grad_near, out_all = lax.optimization_barrier((attended, grad_near, out_all))
    out_own = [
        jnp.concatenate([item.reshape(-1, slab, width) for item in out_all[2 * way : 2 * way + 2]])
        for way in every
    ]
    out_own = jnp.stack(out_own, axis=1).reshape(width // 2, width)
    out_other = core_swap(out_own)
    device = jnp.stack([me, core])
    rows_own, rows_other = arrange(
        slab, device, exchange([rows_of(attended, way) for way in every])
    )
    middle = rows + dot(rows_own, out_own) + dot(rows_other, out_other) + out_bias

    unit_mid, scale_mid = unit_rows(middle)
    normed_mid = gather_rows((unit_mid * ff_gain + ff_shift).astype(bf16))
    normed_mid, grad_near = lax.optimization_barrier((normed_mid, grad_near))
    grad_out_all = jnp.concatenate(gather_far(grad_near), axis=0)
    inner = dot(normed_mid, exp_weight) + exp_bias
    cumulative = (1.0 + lax.erf(inner * 0.7071067811865476)) * 0.5
    active = (inner * cumulative).astype(bf16)
    con_term = dot(active, grad_out_all, ((0,), (0,))).astype(bf16)
    con_term, con_weight = lax.optimization_barrier((con_term, con_weight))
    con_sum = scatter_dp(con_term)
    grad_active = dot(grad_out_all, con_weight, ((1,), (1,)))
    density = jnp.exp(-0.5 * inner * inner) * 0.3989422804014327
    grad_inner = (grad_active * (cumulative + inner * density)).astype(bf16)
    far, near = split_rows(grad_inner, exp_weight, ((1,), (1,)))
    exp_term = dot(normed_mid, grad_inner, ((0,), (0,))).astype(bf16)
    exp_bias_term = jnp.sum(grad_inner.astype(f32), axis=0)
    grad_normed_mid = scatter_rows(far, near)
    exp_term, grad_normed_mid = lax.optimization_barrier((exp_term, grad_normed_mid))
    exp_sum = scatter_dp(exp_term)
    grad_mid_norm, ff_gain_term, ff_shift_term = norm_backward(
        grad_normed_mid, unit_mid, scale_mid, ff_gain
    )
    grad_out_full = grad_out.astype(f32)
    grad_middle = grad_out_full + grad_mid_norm
    grad_branch = grad_middle.astype(bf16)

    grad_own = dot(grad_branch, out_own, ((1,), (1,)))
    grad_other = dot(grad_branch, out_other, ((1,), (1,)))
    grad_heads = disarrange(slab, device, grad_own, grad_other, ways)
    grad_heads, active, grad_branch = lax.optimization_barrier((grad_heads, active, grad_branch))
    grad_heads = jnp.concatenate(exchange(grad_heads), axis=0)
    give = dot(rows_other, grad_branch, ((0,), (0,))).astype(bf16)
    result = dot(active, con_weight)
    out_term = dot(rows_own, grad_branch, ((0,), (0,))) + core_swap(give).astype(f32)
    grad_heads, out_term, result = lax.optimization_barrier((grad_heads, out_term, result))
    last = (ways - 1) * stretch
    result_first = (scatter_far(result[last:]), scatter_side(result[:last]))
    out_term = out_term.reshape(line, ways, slab, width)
    out_term = [out_term[:, way].reshape(line * slab, width) for way in every]
    out_near = jnp.concatenate(out_term[:-1], axis=0)
    out_first = (scatter_far(out_term[-1]), scatter_side(out_near))
    grad_projected = jnp.concatenate(
        attend_backward(stretch, me_array, probs, projected, grad_heads), axis=1
    )
    qkv_term = dot(normed_low, grad_projected, ((0,), (0,))).astype(bf16)
    qkv_term, con_sum, grad_projected, out_first = lax.optimization_barrier(
        (qkv_term, con_sum, grad_projected, out_first)
    )
    far = dot(grad_projected[last:], qkv_weight, ((1,), (1,))).astype(bf16)
    far, grad_projected = lax.optimization_barrier((far, grad_projected))
    near = dot(grad_projected[:last], qkv_weight, ((1,), (1,)))
    first = (scatter_far(far), scatter_side(near))
    near, out_first, result_first, exp_sum = lax.optimization_barrier(
        (near, out_first, result_first, exp_sum)
    )
    exp_grad = own_rows(exp_sum, groups)
    grad_normed_in = scatter_near(near, *first)
    out_term = scatter_near(out_near, *out_first).astype(bf16)
    result = scatter_near(result[:last], *result_first)
    layer_output = (middle + result + con_bias).astype(bf16)[None]
    grad_normed_in, exp_grad = lax.optimization_barrier((grad_normed_in, exp_grad))
    qkv_sum = scatter_dp(qkv_term)
    grad_normed_in, qkv_sum = lax.optimization_barrier((grad_normed_in, qkv_sum))
    grad_in_norm, att_gain_term, att_shift_term = norm_backward(
        grad_normed_in, unit_in, scale_in, att_gain
    )
    input_grad = (grad_middle + grad_in_norm).astype(bf16)[None]

    bias_sums = jnp.sum(grad_projected.astype(f32), axis=0).reshape(3, features)
    qv_term = lax.dynamic_update_slice(
        jnp.zeros((2, ways, features), f32),
        jnp.stack([bias_sums[0], bias_sums[2]])[:, None],
        (0, me, 0),
    ).reshape(-1)
    exp_term = lax.dynamic_update_slice(
        jnp.zeros((groups, ways, inner_slab), f32),
        exp_bias_term.reshape(groups, 1, inner_slab),
        (0, me, 0),
    ).reshape(-1)
    terms = (
        att_gain_term,
        att_shift_term,
        jnp.sum(grad_branch.astype(f32), axis=0),
        ff_gain_term,
        ff_shift_term,
        jnp.sum(grad_out_full, axis=0),
        qv_term,
        exp_term,
    )
    count = groups * ways
    sums = jnp.concatenate([item.reshape(count, -1) for item in terms], axis=1)
    out_grad = halving(out_term.reshape(line, slab, width), "dp", bits_of(groups)[:0:-1])
    out_grad = out_grad[0].astype(f32)
    sums = halving(sums, "dp", bits_of(groups)[::-1])
    sums = halving(sums, "ctx", bits_of(ways)[::-1]).reshape(-1)
    qkv_grad = own_rows(qkv_sum, 3)
    own, at = [], 0
    for item in small:
        own.append(sums[at : at + item.shape[0]])
        at += item.shape[0]
    return (
        layer_output,
        input_grad,
        own[0],
        own[1],
        qkv_grad,
        own[6],
        out_grad,
        own[2],
        own[3],
        own[4],
        exp_grad,
        own[7],
        con_sum.astype(f32),
        own[5],
    )


def solution(mesh):
    tokens = P("dp", "ctx", None)
    vector = P(ALL)
    matrix = P(ALL, None)
    in_specs = (
        tokens,
        P("dp", "ctx"),
        vector,
        vector,
        matrix,
        vector,
        matrix,
        vector,
        vector,
        vector,
        matrix,
        vector,
        matrix,
        vector,
        tokens,
    )
    out_specs = (
        tokens,
        tokens,
        vector,
        vector,
        matrix,
        vector,
        matrix,
        vector,
        vector,
        vector,
        matrix,
        vector,
        matrix,
        vector,
    )
    return jax.shard_map(shards, mesh=mesh, in_specs=in_specs, out_specs=out_specs, check_vma=False)
```

```python
import functools

import jax
import jax.numpy as jnp
from jax import lax
from jax.experimental import pallas as pl
from jax.experimental.pallas import tpu as pltpu
from jax.sharding import PartitionSpec as P

HEADS = 32
HEAD_DIM = 64
PAIR = 2 * HEAD_DIM

bf16 = jnp.bfloat16
f32 = jnp.float32
epsilon = 1e-05


def unit_rows(value):
    mean = jnp.mean(value, axis=-1, keepdims=True)
    centred = value - mean
    scale = lax.rsqrt(jnp.mean(centred * centred, axis=-1, keepdims=True) + epsilon)
    return centred * scale, scale


def norm_backward(grad, unit, scale, gain):
    scaled = grad * gain
    level = jnp.mean(scaled, axis=-1, keepdims=True)
    along = jnp.mean(scaled * unit, axis=-1, keepdims=True)
    return (
        scale * (scaled - level - unit * along),
        jnp.sum(grad * unit, axis=0),
        jnp.sum(grad, axis=0),
    )


def dot(left, right, contract=((1,), (0,))):
    return lax.dot_general(left, right, (contract, ((), ())), preferred_element_type=f32)


def lane_mask(half):
    lane = lax.broadcasted_iota(jnp.int32, (1, PAIR), 1)
    return (lane >= HEAD_DIM) if half else (lane < HEAD_DIM)


def stretch_rows(me_ref, index, block):
    return pl.ds(pl.multiple_of((index ^ me_ref[0]) * block, block), block)


def in_order(me_ref, source, target, block):
    for index in range(source.shape[0] // block):
        target[pl.ds(index * block, block), :] = source[stretch_rows(me_ref, index, block), :]


def attend_forward_kernel(
    block, me_ref, slope_ref, start_ref, q_ref, k_in, v_in, out_ref, probs_ref, k_ref, v_ref
):
    length = q_ref.shape[0]
    pair = pl.program_id(0)
    in_order(me_ref, k_in, k_ref, block)
    in_order(me_ref, v_in, v_ref, block)
    for index in range(length // block):
        rows = stretch_rows(me_ref, index, block)
        place = pl.ds(index * block, block)
        span = (index + 1) * block
        starts = start_ref[rows, :]
        q_place = index * block + lax.broadcasted_iota(jnp.int32, (block, span), 0)
        k_place = lax.broadcasted_iota(jnp.int32, (block, span), 1)
        visible = (k_place >= starts) & (k_place <= q_place)
        k_row = lax.broadcasted_iota(jnp.int32, (1, span), 1).astype(f32)
        mixed = []
        for half in range(2):
            slope = slope_ref[pair * 2 + half]
            query = jnp.where(lane_mask(half), q_ref[rows, :] * bf16(0.125), bf16(0))
            scores = dot(query, k_ref[:span, :], ((1,), (1,))) + slope * k_row
            scores = jnp.where(visible, scores, -1e30)
            top = jnp.max(scores, axis=-1, keepdims=True)
            weights = jnp.exp(scores - top)
            total = jnp.sum(weights, axis=-1, keepdims=True)
            probs = (weights * (1.0 / total)).astype(bf16)
            probs_ref[half, place, :span] = probs
            mixed.append(dot(probs, v_ref[:span, :]))
        out_ref[rows, :] = jnp.where(lane_mask(0), mixed[0], mixed[1]).astype(bf16)


def attend_backward_kernel(
    block, me_ref, probs_ref, q_ref, k_in, v_in, g_ref, dq_ref, dk_ref, dv_ref, k_ref, v_ref, dk_sum, dv_sum
):
    length = q_ref.shape[0]
    in_order(me_ref, k_in, k_ref, block)
    in_order(me_ref, v_in, v_ref, block)
    dk_sum[...] = jnp.zeros_like(dk_sum)
    dv_sum[...] = jnp.zeros_like(dv_sum)
    for index in range(length // block):
        rows = stretch_rows(me_ref, index, block)
        place = pl.ds(index * block, block)
        span = (index + 1) * block
        parts = []
        for half in range(2):
            mask = lane_mask(half)
            grad = jnp.where(mask, g_ref[rows, :], bf16(0))
            query = jnp.where(mask, q_ref[rows, :] * bf16(0.125), bf16(0))
            probs_low = probs_ref[half, place, :span]
            probs = probs_low.astype(f32)
            grad_probs = dot(grad, v_ref[:span, :], ((1,), (1,)))
            along = jnp.sum(probs * grad_probs, axis=-1, keepdims=True)
            grad_scores = (probs * (grad_probs - along)).astype(bf16)
            parts.append(dot(grad_scores, k_ref[:span, :]))
            dk_sum[:span, :] += dot(grad_scores, query, ((0,), (0,)))
            dv_sum[:span, :] += dot(probs_low, grad, ((0,), (0,)))
        dq_ref[rows, :] = (jnp.where(lane_mask(0), parts[0], parts[1]) * 0.125).astype(bf16)
    for index in range(length // block):
        rows = stretch_rows(me_ref, index, block)
        place = pl.ds(index * block, block)
        dk_ref[rows, :] = dk_sum[place, :].astype(bf16)
        dv_ref[rows, :] = dv_sum[place, :].astype(bf16)


def attend_forward(block, me, slopes, starts, projected):
    length = projected.shape[0]
    heads = projected.shape[1] // (3 * HEAD_DIM)
    pairs = heads // 2
    column = lambda first: pl.BlockSpec((length, PAIR), lambda p: (0, first + p))
    return pl.pallas_call(
        functools.partial(attend_forward_kernel, block),
        grid=(pairs,),
        in_specs=[
            pl.BlockSpec(memory_space=pltpu.SMEM),
            pl.BlockSpec(memory_space=pltpu.SMEM),
            pl.BlockSpec((length, 1), lambda p: (0, 0)),
            column(0),
            column(pairs),
            column(2 * pairs),
        ],
        out_specs=[column(0), pl.BlockSpec((2, length, length), lambda p: (p, 0, 0))],
        out_shape=[
            jax.ShapeDtypeStruct((length, heads * HEAD_DIM), bf16),
            jax.ShapeDtypeStruct((heads, length, length), bf16),
        ],
        scratch_shapes=[pltpu.VMEM((length, PAIR), bf16), pltpu.VMEM((length, PAIR), bf16)],
        compiler_params=pltpu.CompilerParams(vmem_limit_bytes=50 * 2**20),
        cost_estimate=pl.CostEstimate(
            flops=4 * heads * length * length * PAIR,
            bytes_accessed=2 * heads * length * length,
            transcendentals=heads * length * length,
        ),
        name="attend_forward",
    )(me, slopes, starts, projected, projected, projected)


def attend_backward(block, me, probs, projected, grad):
    length = projected.shape[0]
    heads = projected.shape[1] // (3 * HEAD_DIM)
    pairs = heads // 2
    column = lambda first: pl.BlockSpec((length, PAIR), lambda p: (0, first + p))
    shape = jax.ShapeDtypeStruct((length, heads * HEAD_DIM), bf16)
    return pl.pallas_call(
        functools.partial(attend_backward_kernel, block),
        grid=(pairs,),
        in_specs=[
            pl.BlockSpec(memory_space=pltpu.SMEM),
            pl.BlockSpec((2, length, length), lambda p: (p, 0, 0)),
            column(0),
            column(pairs),
            column(2 * pairs),
            column(0),
        ],
        out_specs=[column(0), column(0), column(0)],
        out_shape=[shape, shape, shape],
        scratch_shapes=[
            pltpu.VMEM((length, PAIR), bf16),
            pltpu.VMEM((length, PAIR), bf16),
            pltpu.VMEM((length, PAIR), f32),
            pltpu.VMEM((length, PAIR), f32),
        ],
        compiler_params=pltpu.CompilerParams(vmem_limit_bytes=50 * 2**20),
        cost_estimate=pl.CostEstimate(
            flops=8 * heads * length * length * PAIR,
            bytes_accessed=2 * heads * length * length,
            transcendentals=0,
        ),
        name="attend_backward",
    )(me, probs, projected, projected, projected, grad)


def relative_slabs(value, me, ways, slab):
    width = value.shape[1]
    lane = lax.broadcasted_iota(jnp.int32, (1, width), 1)
    bit = 1
    while bit < ways:
        size = bit * slab
        upper, lower = pltpu.roll(value, size, 1), pltpu.roll(value, width - size, 1)
        swapped = jnp.where((lane & size) != 0, upper, lower)
        value = jnp.where((me & bit) != 0, swapped, value)
        bit *= 2
    return value


def arrange_kernel(slab, spot_ref, *refs):
    *part_refs, own_ref, other_ref, whole = refs
    ways = len(part_refs)
    me, core = spot_ref[0], spot_ref[1]
    features, width = part_refs[0].shape[1], whole.shape[1]
    for way, ref in enumerate(part_refs):
        place = pl.ds(pl.multiple_of((me ^ way) * features, 128), features)
        whole[:, place] = ref[...].astype(f32)
    whole[...] = relative_slabs(whole[...], me, ways, slab)
    size = ways * slab
    for n in range(width // (2 * size)):
        for which, ref in ((0, own_ref), (1, other_ref)):
            place = pl.ds(pl.multiple_of((2 * n + (core ^ which)) * size, 128), size)
            ref[:, n * size : (n + 1) * size] = whole[:, place].astype(bf16)


def disarrange_kernel(slab, spot_ref, own_ref, other_ref, *refs):
    *part_refs, whole = refs
    ways = len(part_refs)
    me, core = spot_ref[0], spot_ref[1]
    features, width = part_refs[0].shape[1], whole.shape[1]
    size = ways * slab
    for n in range(width // (2 * size)):
        for which, ref in ((0, own_ref), (1, other_ref)):
            place = pl.ds(pl.multiple_of((2 * n + (core ^ which)) * size, 128), size)
            whole[:, place] = ref[:, n * size : (n + 1) * size]
    whole[...] = relative_slabs(whole[...], me, ways, slab)
    for way, ref in enumerate(part_refs):
        place = pl.ds(pl.multiple_of((me ^ way) * features, 128), features)
        ref[...] = whole[:, place].astype(bf16)


def arrange(slab, spot, parts):
    rows, features = parts[0].shape
    width = features * len(parts)
    vmem = pl.BlockSpec(memory_space=pltpu.VMEM)
    half = jax.ShapeDtypeStruct((rows, width // 2), bf16)
    return pl.pallas_call(
        functools.partial(arrange_kernel, slab),
        in_specs=[pl.BlockSpec(memory_space=pltpu.SMEM)] + [vmem] * len(parts),
        out_specs=[vmem, vmem],
        out_shape=[half, half],
        scratch_shapes=[pltpu.VMEM((rows, width), f32)],
        compiler_params=pltpu.CompilerParams(vmem_limit_bytes=32 * 2**20),
        cost_estimate=pl.CostEstimate(
            flops=16 * rows * width, bytes_accessed=4 * rows * width, transcendentals=0
        ),
        name="arrange",
    )(spot, *parts)


def disarrange(slab, spot, own, other, ways):
    rows, width = own.shape[0], 2 * own.shape[1]
    vmem = pl.BlockSpec(memory_space=pltpu.VMEM)
    part = jax.ShapeDtypeStruct((rows, width // ways), bf16)
    return pl.pallas_call(
        functools.partial(disarrange_kernel, slab),
        in_specs=[pl.BlockSpec(memory_space=pltpu.SMEM), vmem, vmem],
        out_specs=[vmem] * ways,
        out_shape=[part] * ways,
        scratch_shapes=[pltpu.VMEM((rows, width), f32)],
        compiler_params=pltpu.CompilerParams(vmem_limit_bytes=32 * 2**20),
        cost_estimate=pl.CostEstimate(
            flops=16 * rows * width, bytes_accessed=6 * rows * width, transcendentals=0
        ),
        name="disarrange",
    )(spot, own, other)


def lay_kernel(count, spot_ref, *refs):
    *part_refs, out_ref = refs
    ways = len(part_refs)
    size = part_refs[0].shape[1] // count
    for way, ref in enumerate(part_refs):
        for n in range(count):
            place = pl.multiple_of((n * ways + (way ^ spot_ref[0])) * size, 128)
            out_ref[:, pl.ds(place, size)] = ref[:, n * size : (n + 1) * size].astype(f32)


def lay(count, spot, parts):
    rows, width = parts[0].shape[0], parts[0].shape[1] * len(parts)
    vmem = pl.BlockSpec(memory_space=pltpu.VMEM)
    return pl.pallas_call(
        functools.partial(lay_kernel, count),
        in_specs=[pl.BlockSpec(memory_space=pltpu.SMEM)] + [vmem] * len(parts),
        out_specs=vmem,
        out_shape=jax.ShapeDtypeStruct((rows, width), f32),
        compiler_params=pltpu.CompilerParams(vmem_limit_bytes=32 * 2**20),
        cost_estimate=pl.CostEstimate(
            flops=0, bytes_accessed=6 * rows * width, transcendentals=0
        ),
        name="lay",
    )(spot, *parts)


def pack_kernel(*refs):
    *item_refs, out_ref = refs
    width = out_ref.shape[1]
    rows = []
    for ref in item_refs:
        row, rest = ref[...].astype(f32), width - ref.shape[1]
        rows.append(jnp.concatenate([row, jnp.zeros((1, rest), f32)], axis=1) if rest else row)
    rest = out_ref.shape[0] - len(rows)
    rows.append(jnp.zeros((rest, width), f32))
    out_ref[...] = jnp.concatenate(rows, axis=0).astype(bf16)


def pack(items, width):
    vmem = pl.BlockSpec(memory_space=pltpu.VMEM)
    return pl.pallas_call(
        pack_kernel,
        in_specs=[vmem] * len(items),
        out_specs=vmem,
        out_shape=jax.ShapeDtypeStruct((16, width), bf16),
        name="pack",
    )(*[item[None] for item in items])


ALL = ("dp", "ctx")


def hop(value, way):
    ways = lax.axis_size("ctx")
    return lax.ppermute(value, "ctx", [(c, c ^ way) for c in range(ways)])


def gather_near(value):
    ways, half = lax.axis_size("ctx"), value.shape[0] // 2
    halves = [value[:half], value[half:]]
    return [halves] + [
        [hop(item, way) for item in halves] for way in range(1, 3 if ways == 4 else ways)
    ]


def gather_far(parts):
    if lax.axis_size("ctx") == 4:
        parts = parts + [[hop(parts[1][0], 2), hop(parts[2][1], 1)]]
    return [item for halves in parts for item in halves]


def gather_rows(value):
    return jnp.concatenate(gather_far(gather_near(value)), axis=0)


def halves_of(near, ways):
    half = near.shape[0] // (2 * ways - 2)
    return [near[n * half : (n + 1) * half] for n in range(2 * ways - 2)]


def scatter_far(far):
    far, half = far.astype(bf16), far.shape[0] // 2
    if lax.axis_size("ctx") != 4:
        return [far[:half], far[half:]]
    return [hop(far[:half], 1), hop(far[half:], 2)]


def scatter_side(near):
    ways = lax.axis_size("ctx")
    near = halves_of(near, ways)
    if ways != 4:
        return [item.astype(bf16) for item in near[2:4]]
    return [hop(near[2].astype(bf16), 1), hop(near[5].astype(bf16), 2)]


def scatter_near(near, far, side):
    ways = lax.axis_size("ctx")
    near = halves_of(near, ways)
    total = near[:2]
    if ways != 4:
        for n, part in enumerate(side + near[4:] + far):
            total[n % 2] = total[n % 2] + hop(part.astype(bf16), 1 + n // 2).astype(f32)
    else:
        upper, lower = far
        one = hop((near[3] + lower.astype(f32)).astype(bf16), 1)
        two = hop((near[4] + upper.astype(f32)).astype(bf16), 2)
        total[0] = total[0] + side[0].astype(f32) + two.astype(f32)
        total[1] = total[1] + side[1].astype(f32) + one.astype(f32)
    return jnp.concatenate(total, axis=0)


def scatter_rows(far, near):
    return scatter_near(near, scatter_far(far), scatter_side(near))


def exchange(pieces):
    return [pieces[0]] + [hop(piece, way) for way, piece in enumerate(pieces) if way]


def place_parts(parts, axis):
    me = lax.axis_index("ctx")
    return jnp.concatenate(
        [lax.select_n(me ^ place, *parts) for place in range(len(parts))], axis=axis
    )


def doubling(value, axis, bits):
    size, me = lax.axis_size(axis), lax.axis_index(axis)
    for bit in bits:
        other = lax.ppermute(value, axis, [(d, d ^ bit) for d in range(size)])
        upper = (me & bit) != 0
        value = jnp.where(
            upper,
            jnp.concatenate([other, value], axis=0),
            jnp.concatenate([value, other], axis=0),
        )
    return value


def halving(value, axis, bits):
    size, me = lax.axis_size(axis), lax.axis_index(axis)
    for bit in bits:
        half = value.shape[0] // 2
        upper = (me & bit) != 0
        keep = jnp.where(upper, value[half:], value[:half])
        give = jnp.where(upper, value[:half], value[half:])
        value = keep + lax.ppermute(give, axis, [(d, d ^ bit) for d in range(size)])
    return value


def bits_of(size):
    return [1 << n for n in range(size.bit_length() - 1)]


def core_swap(value):
    groups = lax.axis_size("dp")
    return lax.ppermute(value, "dp", [(d, d ^ 1) for d in range(groups)])


def shards(
    residual_in,
    document_ids,
    attention_gain,
    attention_shift,
    query_key_value,
    query_value_bias,
    output_weight,
    output_bias,
    feedforward_gain,
    feedforward_shift,
    expand_weight,
    expand_bias,
    contract_weight,
    contract_bias,
    output_grad,
):
    groups, ways = lax.axis_size("dp"), lax.axis_size("ctx")
    me_dp, me = lax.axis_index("dp"), lax.axis_index("ctx")
    seqs, stretch, width = residual_in.shape
    assert seqs == 1
    length = stretch * ways
    slab = query_key_value.shape[0]
    inner_slab = contract_weight.shape[0]
    features = width // ways
    heads = HEADS // ways
    line, core, spot = groups // 2, me_dp & 1, me_dp >> 1

    def rows_of(value, way):
        return value[way * stretch : (way + 1) * stretch]

    def pieces_of(value, count):
        size = value.shape[1] // (count * ways)
        absolute = [
            jnp.concatenate(
                [value[:, (n * ways + p) * size : (n * ways + p + 1) * size] for n in range(count)], 1
            )
            for p in range(ways)
        ]
        return [lax.select_n(me ^ way, *absolute) for way in range(ways)]

    def gather_dp(value):
        return lax.all_gather(value, "dp", axis=0, tiled=True)

    def core_columns(value, core):
        size = value.shape[1] // groups
        return jnp.concatenate(
            [lax.dynamic_slice_in_dim(value, (2 * n + core) * size, size, 1) for n in range(line)], 1
        )

    def core_term(left, right):
        give = dot(core_columns(left, core ^ 1), right, ((0,), (0,))).astype(bf16)
        keep = dot(core_columns(left, core), right, ((0,), (0,)))
        return (keep + core_swap(give).astype(f32)).astype(bf16)

    def scatter_dp(value):
        return lax.psum_scatter(value, "dp", scatter_dimension=0, tiled=True)

    def scatter_line(value):
        lines = [[2 * n + core for n in range(line)] for core in range(2)]
        return lax.psum_scatter(
            value, "dp", scatter_dimension=0, tiled=True, axis_index_groups=lines
        )

    def split_rows(left, right, contract):
        last = (ways - 1) * stretch
        return dot(left[last:], right, contract), dot(left[:last], right, contract)

    def own_rows(grad, count):
        pieces = [
            lax.dynamic_slice_in_dim(grad, (me ^ way) * slab, slab, 0) for way in range(ways)
        ]
        parts = exchange(pieces)
        size = grad.shape[1] // count
        if size % 128 == 0:
            return lay(count, me.reshape(1), parts)
        parts = [lax.select_n(me ^ place, *parts) for place in range(ways)]
        return jnp.concatenate(
            [part[:, n * size : (n + 1) * size] for n in range(count) for part in parts], axis=1
        ).astype(f32)

    small = (
        attention_gain,
        attention_shift,
        output_bias,
        feedforward_gain,
        feedforward_shift,
        contract_bias,
        query_value_bias,
        expand_bias,
    )
    every = range(ways)
    begin = (document_ids[0] - me_dp * length).reshape(-1, inner_slab)
    kinds, lines = len(small), begin.shape[0]
    begin = [*(begin >> 5).astype(bf16), *(begin & 31).astype(bf16)]
    qkv_parts = exchange(pieces_of(query_key_value, 3))
    out_block = jnp.concatenate([output_weight, pack([*small, *begin], width)], axis=0)
    out_parts = [out_block] + [
        lax.ppermute(out_block, "dp", [(d, (d + 2 * n) % groups) for d in range(groups)])
        for n in range(1, line)
    ]
    block = residual_in[0]
    qkv_parts, out_parts, expand_weight, block = lax.optimization_barrier(
        (qkv_parts, out_parts, expand_weight, block)
    )
    qkv_weight = gather_dp(place_parts(qkv_parts, 0))
    packs = [part[slab:, :inner_slab] for part in out_parts]
    packs = [lax.select_n((spot - n + line) % line, *packs) for n in range(line)]
    other = core_swap(jnp.concatenate(packs, axis=1))
    packed = []
    for n, mine in enumerate(packs):
        theirs = other[:, n * inner_slab : (n + 1) * inner_slab]
        packed += [jnp.where(core == 0, mine, theirs), jnp.where(core == 0, theirs, mine)]
    packed = jnp.concatenate(packed, axis=1)
    exp_parts = exchange(
        [jnp.concatenate([piece, packed], axis=0) for piece in pieces_of(expand_weight, groups)]
    )
    block_all = gather_rows(block)
    out_mine = jnp.concatenate(
        [
            lax.select_n((spot - n + line) % line, *[part[:slab] for part in out_parts])
            for n in range(line)
        ],
        axis=0,
    )
    block_all, exp_parts, out_mine = lax.optimization_barrier((block_all, exp_parts, out_mine))
    packs = [part[slab:] for part in exp_parts]
    exp_parts = [part[:slab] for part in exp_parts]
    begin = [
        lax.dynamic_slice_in_dim(part[kinds : kinds + 2 * lines], me_dp * inner_slab, inner_slab, 1)
        for part in packs
    ]
    begin = [32.0 * item[:lines].astype(f32) + item[lines:].astype(f32) for item in begin]
    starts = jnp.concatenate(begin, axis=0).astype(jnp.int32).reshape(length, 1)
    packed = [part[:kinds].astype(f32).reshape(kinds, groups, inner_slab) for part in packs]
    packed = jnp.stack([lax.select_n(me ^ place, *packed) for place in every], axis=2)
    whole = [packed[n, :, :, : item.shape[0]].reshape(-1) for n, item in enumerate(small)]
    att_gain, att_shift, out_bias, ff_gain, ff_shift, con_bias, qv_bias, exp_bias = whole
    exp_bias = lax.dynamic_index_in_dim(
        exp_bias.reshape(groups, ways, inner_slab), me, 1, keepdims=False
    ).reshape(-1)
    qv_bias = lax.dynamic_index_in_dim(qv_bias.reshape(2, ways, features), me, 1, keepdims=False)
    exp_weight = gather_dp(place_parts(exp_parts, 0))
    con_weight = gather_dp(contract_weight)
    out_near = gather_near(out_mine)
    grad_out = output_grad[0]
    slopes = jnp.exp2(
        -8.0 * ((me * heads + jnp.arange(heads, dtype=jnp.int32)).astype(f32) + 1.0) / HEADS
    )

    rows = block.astype(f32)
    unit_in, scale_in = unit_rows(rows)
    normed_low = (unit_rows(block_all.astype(f32))[0] * att_gain + att_shift).astype(bf16)
    bias = jnp.concatenate([qv_bias[0], jnp.zeros((features,), f32), qv_bias[1]])
    projected = (dot(normed_low, qkv_weight) + bias).astype(bf16)
    projected, out_near = lax.optimization_barrier((projected, out_near))
    out_all = gather_far(out_near)
    grad_near = gather_near(grad_out)
    me_array = me.reshape(1)
    attended, probs = attend_forward(stretch, me_array, slopes, starts, projected)
    attended, grad_near, out_all = lax.optimization_barrier((attended, grad_near, out_all))
    out_own = [
        jnp.concatenate([item.reshape(-1, slab, width) for item in out_all[2 * way : 2 * way + 2]])
        for way in every
    ]
    out_own = jnp.stack(out_own, axis=1).reshape(width // 2, width)
    out_other = core_swap(out_own)
    device = jnp.stack([me, core])
    rows_own, rows_other = arrange(
        slab, device, exchange([rows_of(attended, way) for way in every])
    )
    middle = rows + dot(rows_own, out_own) + dot(rows_other, out_other) + out_bias

    unit_mid, scale_mid = unit_rows(middle)
    normed_mid = gather_rows((unit_mid * ff_gain + ff_shift).astype(bf16))
    normed_mid, grad_near = lax.optimization_barrier((normed_mid, grad_near))
    grad_out_all = jnp.concatenate(gather_far(grad_near), axis=0)
    inner = dot(normed_mid, exp_weight) + exp_bias
    cumulative = (1.0 + lax.erf(inner * 0.7071067811865476)) * 0.5
    active = (inner * cumulative).astype(bf16)
    con_term = dot(active, grad_out_all, ((0,), (0,))).astype(bf16)
    con_term, con_weight = lax.optimization_barrier((con_term, con_weight))
    con_sum = scatter_dp(con_term)
    grad_active = dot(grad_out_all, con_weight, ((1,), (1,)))
    density = jnp.exp(-0.5 * inner * inner) * 0.3989422804014327
    grad_inner = (grad_active * (cumulative + inner * density)).astype(bf16)
    far, near = split_rows(grad_inner, exp_weight, ((1,), (1,)))
    exp_term = dot(normed_mid, grad_inner, ((0,), (0,))).astype(bf16)
    exp_bias_term = jnp.sum(grad_inner.astype(f32), axis=0)
    grad_normed_mid = scatter_rows(far, near)
    exp_term, grad_normed_mid = lax.optimization_barrier((exp_term, grad_normed_mid))
    exp_sum = scatter_dp(exp_term)
    grad_mid_norm, ff_gain_term, ff_shift_term = norm_backward(
        grad_normed_mid, unit_mid, scale_mid, ff_gain
    )
    grad_out_full = grad_out.astype(f32)
    grad_middle = grad_out_full + grad_mid_norm
    grad_branch = grad_middle.astype(bf16)

    grad_own = dot(grad_branch, out_own, ((1,), (1,)))
    grad_other = dot(grad_branch, out_other, ((1,), (1,)))
    grad_heads = disarrange(slab, device, grad_own, grad_other, ways)
    grad_heads, active, grad_branch = lax.optimization_barrier((grad_heads, active, grad_branch))
    grad_heads = jnp.concatenate(exchange(grad_heads), axis=0)
    give = dot(rows_other, grad_branch, ((0,), (0,))).astype(bf16)
    result = dot(active, con_weight)
    out_term = dot(rows_own, grad_branch, ((0,), (0,))) + core_swap(give).astype(f32)
    grad_heads, out_term, result = lax.optimization_barrier((grad_heads, out_term, result))
    last = (ways - 1) * stretch
    result_first = (scatter_far(result[last:]), scatter_side(result[:last]))
    out_term = out_term.reshape(line, ways, slab, width)
    out_term = [out_term[:, way].reshape(line * slab, width) for way in every]
    out_near = jnp.concatenate(out_term[:-1], axis=0)
    out_first = (scatter_far(out_term[-1]), scatter_side(out_near))
    grad_projected = jnp.concatenate(
        attend_backward(stretch, me_array, probs, projected, grad_heads), axis=1
    )
    qkv_term = dot(normed_low, grad_projected, ((0,), (0,))).astype(bf16)
    qkv_term, con_sum, grad_projected, out_first = lax.optimization_barrier(
        (qkv_term, con_sum, grad_projected, out_first)
    )
    far = dot(grad_projected[last:], qkv_weight, ((1,), (1,))).astype(bf16)
    far, grad_projected = lax.optimization_barrier((far, grad_projected))
    near = dot(grad_projected[:last], qkv_weight, ((1,), (1,)))
    first = (scatter_far(far), scatter_side(near))
    first, out_first, result_first, exp_sum = lax.optimization_barrier(
        (first, out_first, result_first, exp_sum)
    )
    exp_grad = own_rows(exp_sum, groups)
    grad_normed_in = scatter_near(near, *first)
    out_term = scatter_near(out_near, *out_first).astype(bf16)
    result = scatter_near(result[:last], *result_first)
    layer_output = (middle + result + con_bias).astype(bf16)[None]
    grad_normed_in, exp_grad = lax.optimization_barrier((grad_normed_in, exp_grad))
    qkv_sum = scatter_dp(qkv_term)
    grad_normed_in, qkv_sum = lax.optimization_barrier((grad_normed_in, qkv_sum))
    grad_in_norm, att_gain_term, att_shift_term = norm_backward(
        grad_normed_in, unit_in, scale_in, att_gain
    )
    input_grad = (grad_middle + grad_in_norm).astype(bf16)[None]

    bias_sums = jnp.sum(grad_projected.astype(f32), axis=0).reshape(3, features)
    qv_term = lax.dynamic_update_slice(
        jnp.zeros((2, ways, features), f32),
        jnp.stack([bias_sums[0], bias_sums[2]])[:, None],
        (0, me, 0),
    ).reshape(-1)
    exp_term = lax.dynamic_update_slice(
        jnp.zeros((groups, ways, inner_slab), f32),
        exp_bias_term.reshape(groups, 1, inner_slab),
        (0, me, 0),
    ).reshape(-1)
    terms = (
        att_gain_term,
        att_shift_term,
        jnp.sum(grad_branch.astype(f32), axis=0),
        ff_gain_term,
        ff_shift_term,
        jnp.sum(grad_out_full, axis=0),
        qv_term,
        exp_term,
    )
    count = groups * ways
    sums = jnp.concatenate([item.reshape(count, -1) for item in terms], axis=1)
    out_grad = halving(out_term.reshape(line, slab, width), "dp", bits_of(groups)[:0:-1])
    out_grad = out_grad[0].astype(f32)
    sums = halving(sums, "dp", bits_of(groups)[::-1])
    sums = halving(sums, "ctx", bits_of(ways)[::-1]).reshape(-1)
    qkv_grad = own_rows(qkv_sum, 3)
    own, at = [], 0
    for item in small:
        own.append(sums[at : at + item.shape[0]])
        at += item.shape[0]
    return (
        layer_output,
        input_grad,
        own[0],
        own[1],
        qkv_grad,
        own[6],
        out_grad,
        own[2],
        own[3],
        own[4],
        exp_grad,
        own[7],
        con_sum.astype(f32),
        own[5],
    )


def solution(mesh):
    tokens = P("dp", "ctx", None)
    vector = P(ALL)
    matrix = P(ALL, None)
    in_specs = (
        tokens,
        P("dp", "ctx"),
        vector,
        vector,
        matrix,
        vector,
        matrix,
        vector,
        vector,
        vector,
        matrix,
        vector,
        matrix,
        vector,
        tokens,
    )
    out_specs = (
        tokens,
        tokens,
        vector,
        vector,
        matrix,
        vector,
        matrix,
        vector,
        vector,
        vector,
        matrix,
        vector,
        matrix,
        vector,
    )
    return jax.shard_map(shards, mesh=mesh, in_specs=in_specs, out_specs=out_specs, check_vma=False)
```

```python
import functools

import jax
import jax.numpy as jnp
from jax import lax
from jax.experimental import pallas as pl
from jax.experimental.pallas import tpu as pltpu
from jax.sharding import PartitionSpec as P

HEADS = 32
HEAD_DIM = 64
PAIR = 2 * HEAD_DIM

bf16 = jnp.bfloat16
f32 = jnp.float32
epsilon = 1e-05


def unit_rows(value):
    mean = jnp.mean(value, axis=-1, keepdims=True)
    centred = value - mean
    scale = lax.rsqrt(jnp.mean(centred * centred, axis=-1, keepdims=True) + epsilon)
    return centred * scale, scale


def norm_backward(grad, unit, scale, gain):
    scaled = grad * gain
    level = jnp.mean(scaled, axis=-1, keepdims=True)
    along = jnp.mean(scaled * unit, axis=-1, keepdims=True)
    return (
        scale * (scaled - level - unit * along),
        jnp.sum(grad * unit, axis=0),
        jnp.sum(grad, axis=0),
    )


def dot(left, right, contract=((1,), (0,))):
    return lax.dot_general(left, right, (contract, ((), ())), preferred_element_type=f32)


def lane_mask(half):
    lane = lax.broadcasted_iota(jnp.int32, (1, PAIR), 1)
    return (lane >= HEAD_DIM) if half else (lane < HEAD_DIM)


def stretch_rows(me_ref, index, block):
    return pl.ds(pl.multiple_of((index ^ me_ref[0]) * block, block), block)


def in_order(me_ref, source, target, block):
    for index in range(source.shape[0] // block):
        target[pl.ds(index * block, block), :] = source[stretch_rows(me_ref, index, block), :]


def attend_forward_kernel(
    block, me_ref, slope_ref, start_ref, q_ref, k_in, v_in, out_ref, probs_ref, k_ref, v_ref
):
    length = q_ref.shape[0]
    pair = pl.program_id(0)
    in_order(me_ref, k_in, k_ref, block)
    in_order(me_ref, v_in, v_ref, block)
    for index in range(length // block):
        rows = stretch_rows(me_ref, index, block)
        place = pl.ds(index * block, block)
        span = (index + 1) * block
        starts = start_ref[rows, :]
        q_place = index * block + lax.broadcasted_iota(jnp.int32, (block, span), 0)
        k_place = lax.broadcasted_iota(jnp.int32, (block, span), 1)
        visible = (k_place >= starts) & (k_place <= q_place)
        k_row = lax.broadcasted_iota(jnp.int32, (1, span), 1).astype(f32)
        mixed = []
        for half in range(2):
            slope = slope_ref[pair * 2 + half]
            query = jnp.where(lane_mask(half), q_ref[rows, :] * bf16(0.125), bf16(0))
            scores = dot(query, k_ref[:span, :], ((1,), (1,))) + slope * k_row
            scores = jnp.where(visible, scores, -1e30)
            top = jnp.max(scores, axis=-1, keepdims=True)
            weights = jnp.exp(scores - top)
            total = jnp.sum(weights, axis=-1, keepdims=True)
            probs = (weights * (1.0 / total)).astype(bf16)
            probs_ref[half, place, :span] = probs
            mixed.append(dot(probs, v_ref[:span, :]))
        out_ref[rows, :] = jnp.where(lane_mask(0), mixed[0], mixed[1]).astype(bf16)


def attend_backward_kernel(
    block, me_ref, probs_ref, q_ref, k_in, v_in, g_ref, dq_ref, dk_ref, dv_ref, k_ref, v_ref, dk_sum, dv_sum
):
    length = q_ref.shape[0]
    in_order(me_ref, k_in, k_ref, block)
    in_order(me_ref, v_in, v_ref, block)
    dk_sum[...] = jnp.zeros_like(dk_sum)
    dv_sum[...] = jnp.zeros_like(dv_sum)
    for index in range(length // block):
        rows = stretch_rows(me_ref, index, block)
        place = pl.ds(index * block, block)
        span = (index + 1) * block
        parts = []
        for half in range(2):
            mask = lane_mask(half)
            grad = jnp.where(mask, g_ref[rows, :], bf16(0))
            query = jnp.where(mask, q_ref[rows, :] * bf16(0.125), bf16(0))
            probs_low = probs_ref[half, place, :span]
            probs = probs_low.astype(f32)
            grad_probs = dot(grad, v_ref[:span, :], ((1,), (1,)))
            along = jnp.sum(probs * grad_probs, axis=-1, keepdims=True)
            grad_scores = (probs * (grad_probs - along)).astype(bf16)
            parts.append(dot(grad_scores, k_ref[:span, :]))
            dk_sum[:span, :] += dot(grad_scores, query, ((0,), (0,)))
            dv_sum[:span, :] += dot(probs_low, grad, ((0,), (0,)))
        dq_ref[rows, :] = (jnp.where(lane_mask(0), parts[0], parts[1]) * 0.125).astype(bf16)
    for index in range(length // block):
        rows = stretch_rows(me_ref, index, block)
        place = pl.ds(index * block, block)
        dk_ref[rows, :] = dk_sum[place, :].astype(bf16)
        dv_ref[rows, :] = dv_sum[place, :].astype(bf16)


def attend_forward(block, me, slopes, starts, projected):
    length = projected.shape[0]
    heads = projected.shape[1] // (3 * HEAD_DIM)
    pairs = heads // 2
    column = lambda first: pl.BlockSpec((length, PAIR), lambda p: (0, first + p))
    return pl.pallas_call(
        functools.partial(attend_forward_kernel, block),
        grid=(pairs,),
        in_specs=[
            pl.BlockSpec(memory_space=pltpu.SMEM),
            pl.BlockSpec(memory_space=pltpu.SMEM),
            pl.BlockSpec((length, 1), lambda p: (0, 0)),
            column(0),
            column(pairs),
            column(2 * pairs),
        ],
        out_specs=[column(0), pl.BlockSpec((2, length, length), lambda p: (p, 0, 0))],
        out_shape=[
            jax.ShapeDtypeStruct((length, heads * HEAD_DIM), bf16),
            jax.ShapeDtypeStruct((heads, length, length), bf16),
        ],
        scratch_shapes=[pltpu.VMEM((length, PAIR), bf16), pltpu.VMEM((length, PAIR), bf16)],
        compiler_params=pltpu.CompilerParams(vmem_limit_bytes=50 * 2**20),
        cost_estimate=pl.CostEstimate(
            flops=4 * heads * length * length * PAIR,
            bytes_accessed=2 * heads * length * length,
            transcendentals=heads * length * length,
        ),
        name="attend_forward",
    )(me, slopes, starts, projected, projected, projected)


def attend_backward(block, me, probs, projected, grad):
    length = projected.shape[0]
    heads = projected.shape[1] // (3 * HEAD_DIM)
    pairs = heads // 2
    column = lambda first: pl.BlockSpec((length, PAIR), lambda p: (0, first + p))
    shape = jax.ShapeDtypeStruct((length, heads * HEAD_DIM), bf16)
    return pl.pallas_call(
        functools.partial(attend_backward_kernel, block),
        grid=(pairs,),
        in_specs=[
            pl.BlockSpec(memory_space=pltpu.SMEM),
            pl.BlockSpec((2, length, length), lambda p: (p, 0, 0)),
            column(0),
            column(pairs),
            column(2 * pairs),
            column(0),
        ],
        out_specs=[column(0), column(0), column(0)],
        out_shape=[shape, shape, shape],
        scratch_shapes=[
            pltpu.VMEM((length, PAIR), bf16),
            pltpu.VMEM((length, PAIR), bf16),
            pltpu.VMEM((length, PAIR), f32),
            pltpu.VMEM((length, PAIR), f32),
        ],
        compiler_params=pltpu.CompilerParams(vmem_limit_bytes=50 * 2**20),
        cost_estimate=pl.CostEstimate(
            flops=8 * heads * length * length * PAIR,
            bytes_accessed=2 * heads * length * length,
            transcendentals=0,
        ),
        name="attend_backward",
    )(me, probs, projected, projected, projected, grad)


def relative_slabs(value, me, ways, slab):
    width = value.shape[1]
    lane = lax.broadcasted_iota(jnp.int32, (1, width), 1)
    bit = 1
    while bit < ways:
        size = bit * slab
        upper, lower = pltpu.roll(value, size, 1), pltpu.roll(value, width - size, 1)
        swapped = jnp.where((lane & size) != 0, upper, lower)
        value = jnp.where((me & bit) != 0, swapped, value)
        bit *= 2
    return value


def arrange_kernel(slab, spot_ref, *refs):
    *part_refs, own_ref, other_ref, whole = refs
    ways = len(part_refs)
    me, core = spot_ref[0], spot_ref[1]
    features, width = part_refs[0].shape[1], whole.shape[1]
    for way, ref in enumerate(part_refs):
        place = pl.ds(pl.multiple_of((me ^ way) * features, 128), features)
        whole[:, place] = ref[...].astype(f32)
    whole[...] = relative_slabs(whole[...], me, ways, slab)
    size = ways * slab
    for n in range(width // (2 * size)):
        for which, ref in ((0, own_ref), (1, other_ref)):
            place = pl.ds(pl.multiple_of((2 * n + (core ^ which)) * size, 128), size)
            ref[:, n * size : (n + 1) * size] = whole[:, place].astype(bf16)


def disarrange_kernel(slab, spot_ref, own_ref, other_ref, *refs):
    *part_refs, whole = refs
    ways = len(part_refs)
    me, core = spot_ref[0], spot_ref[1]
    features, width = part_refs[0].shape[1], whole.shape[1]
    size = ways * slab
    for n in range(width // (2 * size)):
        for which, ref in ((0, own_ref), (1, other_ref)):
            place = pl.ds(pl.multiple_of((2 * n + (core ^ which)) * size, 128), size)
            whole[:, place] = ref[:, n * size : (n + 1) * size]
    whole[...] = relative_slabs(whole[...], me, ways, slab)
    for way, ref in enumerate(part_refs):
        place = pl.ds(pl.multiple_of((me ^ way) * features, 128), features)
        ref[...] = whole[:, place].astype(bf16)


def arrange(slab, spot, parts):
    rows, features = parts[0].shape
    width = features * len(parts)
    vmem = pl.BlockSpec(memory_space=pltpu.VMEM)
    half = jax.ShapeDtypeStruct((rows, width // 2), bf16)
    return pl.pallas_call(
        functools.partial(arrange_kernel, slab),
        in_specs=[pl.BlockSpec(memory_space=pltpu.SMEM)] + [vmem] * len(parts),
        out_specs=[vmem, vmem],
        out_shape=[half, half],
        scratch_shapes=[pltpu.VMEM((rows, width), f32)],
        compiler_params=pltpu.CompilerParams(vmem_limit_bytes=32 * 2**20),
        cost_estimate=pl.CostEstimate(
            flops=16 * rows * width, bytes_accessed=4 * rows * width, transcendentals=0
        ),
        name="arrange",
    )(spot, *parts)


def disarrange(slab, spot, own, other, ways):
    rows, width = own.shape[0], 2 * own.shape[1]
    vmem = pl.BlockSpec(memory_space=pltpu.VMEM)
    part = jax.ShapeDtypeStruct((rows, width // ways), bf16)
    return pl.pallas_call(
        functools.partial(disarrange_kernel, slab),
        in_specs=[pl.BlockSpec(memory_space=pltpu.SMEM), vmem, vmem],
        out_specs=[vmem] * ways,
        out_shape=[part] * ways,
        scratch_shapes=[pltpu.VMEM((rows, width), f32)],
        compiler_params=pltpu.CompilerParams(vmem_limit_bytes=32 * 2**20),
        cost_estimate=pl.CostEstimate(
            flops=16 * rows * width, bytes_accessed=6 * rows * width, transcendentals=0
        ),
        name="disarrange",
    )(spot, own, other)


def lay_kernel(count, spot_ref, *refs):
    *part_refs, out_ref = refs
    ways = len(part_refs)
    size = part_refs[0].shape[1] // count
    for way, ref in enumerate(part_refs):
        for n in range(count):
            place = pl.multiple_of((n * ways + (way ^ spot_ref[0])) * size, 128)
            out_ref[:, pl.ds(place, size)] = ref[:, n * size : (n + 1) * size].astype(f32)


def lay(count, spot, parts):
    rows, width = parts[0].shape[0], parts[0].shape[1] * len(parts)
    vmem = pl.BlockSpec(memory_space=pltpu.VMEM)
    return pl.pallas_call(
        functools.partial(lay_kernel, count),
        in_specs=[pl.BlockSpec(memory_space=pltpu.SMEM)] + [vmem] * len(parts),
        out_specs=vmem,
        out_shape=jax.ShapeDtypeStruct((rows, width), f32),
        compiler_params=pltpu.CompilerParams(vmem_limit_bytes=32 * 2**20),
        cost_estimate=pl.CostEstimate(
            flops=0, bytes_accessed=6 * rows * width, transcendentals=0
        ),
        name="lay",
    )(spot, *parts)


def pack_kernel(*refs):
    *item_refs, out_ref = refs
    width = out_ref.shape[1]
    rows = []
    for ref in item_refs:
        row, rest = ref[...].astype(f32), width - ref.shape[1]
        rows.append(jnp.concatenate([row, jnp.zeros((1, rest), f32)], axis=1) if rest else row)
    rest = out_ref.shape[0] - len(rows)
    rows.append(jnp.zeros((rest, width), f32))
    out_ref[...] = jnp.concatenate(rows, axis=0).astype(bf16)


def pack(items, width):
    vmem = pl.BlockSpec(memory_space=pltpu.VMEM)
    return pl.pallas_call(
        pack_kernel,
        in_specs=[vmem] * len(items),
        out_specs=vmem,
        out_shape=jax.ShapeDtypeStruct((16, width), bf16),
        name="pack",
    )(*[item[None] for item in items])


ALL = ("dp", "ctx")


def hop(value, way):
    ways = lax.axis_size("ctx")
    return lax.ppermute(value, "ctx", [(c, c ^ way) for c in range(ways)])


def gather_near(value):
    ways, half = lax.axis_size("ctx"), value.shape[0] // 2
    halves = [value[:half], value[half:]]
    return [halves] + [
        [hop(item, way) for item in halves] for way in range(1, 3 if ways == 4 else ways)
    ]


def gather_far(parts):
    if lax.axis_size("ctx") == 4:
        parts = parts + [[hop(parts[1][0], 2), hop(parts[2][1], 1)]]
    return [item for halves in parts for item in halves]


def gather_rows(value):
    return jnp.concatenate(gather_far(gather_near(value)), axis=0)


def halves_of(near, ways):
    half = near.shape[0] // (2 * ways - 2)
    return [near[n * half : (n + 1) * half] for n in range(2 * ways - 2)]


def scatter_far(far):
    far, half = far.astype(bf16), far.shape[0] // 2
    if lax.axis_size("ctx") != 4:
        return [far[:half], far[half:]]
    return [hop(far[:half], 1), hop(far[half:], 2)]


def scatter_side(near):
    ways = lax.axis_size("ctx")
    near = halves_of(near, ways)
    if ways != 4:
        return [item.astype(bf16) for item in near[2:4]]
    return [hop(near[2].astype(bf16), 1), hop(near[5].astype(bf16), 2)]


def scatter_near(near, far, side):
    ways = lax.axis_size("ctx")
    near = halves_of(near, ways)
    total = near[:2]
    if ways != 4:
        for n, part in enumerate(side + near[4:] + far):
            total[n % 2] = total[n % 2] + hop(part.astype(bf16), 1 + n // 2).astype(f32)
    else:
        upper, lower = far
        one = hop((near[3] + lower.astype(f32)).astype(bf16), 1)
        two = hop((near[4] + upper.astype(f32)).astype(bf16), 2)
        total[0] = total[0] + side[0].astype(f32) + two.astype(f32)
        total[1] = total[1] + side[1].astype(f32) + one.astype(f32)
    return jnp.concatenate(total, axis=0)


def scatter_rows(far, near):
    return scatter_near(near, scatter_far(far), scatter_side(near))


def exchange(pieces):
    return [pieces[0]] + [hop(piece, way) for way, piece in enumerate(pieces) if way]


def place_parts(parts, axis):
    me = lax.axis_index("ctx")
    return jnp.concatenate(
        [lax.select_n(me ^ place, *parts) for place in range(len(parts))], axis=axis
    )


def doubling(value, axis, bits):
    size, me = lax.axis_size(axis), lax.axis_index(axis)
    for bit in bits:
        other = lax.ppermute(value, axis, [(d, d ^ bit) for d in range(size)])
        upper = (me & bit) != 0
        value = jnp.where(
            upper,
            jnp.concatenate([other, value], axis=0),
            jnp.concatenate([value, other], axis=0),
        )
    return value


def halving(value, axis, bits):
    size, me = lax.axis_size(axis), lax.axis_index(axis)
    for bit in bits:
        half = value.shape[0] // 2
        upper = (me & bit) != 0
        keep = jnp.where(upper, value[half:], value[:half])
        give = jnp.where(upper, value[:half], value[half:])
        value = keep + lax.ppermute(give, axis, [(d, d ^ bit) for d in range(size)])
    return value


def bits_of(size):
    return [1 << n for n in range(size.bit_length() - 1)]


def core_swap(value):
    groups = lax.axis_size("dp")
    return lax.ppermute(value, "dp", [(d, d ^ 1) for d in range(groups)])


def shards(
    residual_in,
    document_ids,
    attention_gain,
    attention_shift,
    query_key_value,
    query_value_bias,
    output_weight,
    output_bias,
    feedforward_gain,
    feedforward_shift,
    expand_weight,
    expand_bias,
    contract_weight,
    contract_bias,
    output_grad,
):
    groups, ways = lax.axis_size("dp"), lax.axis_size("ctx")
    me_dp, me = lax.axis_index("dp"), lax.axis_index("ctx")
    seqs, stretch, width = residual_in.shape
    assert seqs == 1
    length = stretch * ways
    slab = query_key_value.shape[0]
    inner_slab = contract_weight.shape[0]
    features = width // ways
    heads = HEADS // ways
    line, core, spot = groups // 2, me_dp & 1, me_dp >> 1

    def rows_of(value, way):
        return value[way * stretch : (way + 1) * stretch]

    def pieces_of(value, count):
        size = value.shape[1] // (count * ways)
        absolute = [
            jnp.concatenate(
                [value[:, (n * ways + p) * size : (n * ways + p + 1) * size] for n in range(count)], 1
            )
            for p in range(ways)
        ]
        return [lax.select_n(me ^ way, *absolute) for way in range(ways)]

    def gather_dp(value):
        return lax.all_gather(value, "dp", axis=0, tiled=True)

    def core_columns(value, core):
        size = value.shape[1] // groups
        return jnp.concatenate(
            [lax.dynamic_slice_in_dim(value, (2 * n + core) * size, size, 1) for n in range(line)], 1
        )

    def core_term(left, right):
        give = dot(core_columns(left, core ^ 1), right, ((0,), (0,))).astype(bf16)
        keep = dot(core_columns(left, core), right, ((0,), (0,)))
        return (keep + core_swap(give).astype(f32)).astype(bf16)

    def scatter_dp(value):
        return lax.psum_scatter(value, "dp", scatter_dimension=0, tiled=True)

    def scatter_line(value):
        lines = [[2 * n + core for n in range(line)] for core in range(2)]
        return lax.psum_scatter(
            value, "dp", scatter_dimension=0, tiled=True, axis_index_groups=lines
        )

    def split_rows(left, right, contract):
        last = (ways - 1) * stretch
        return dot(left[last:], right, contract), dot(left[:last], right, contract)

    def own_rows(grad, count):
        pieces = [
            lax.dynamic_slice_in_dim(grad, (me ^ way) * slab, slab, 0) for way in range(ways)
        ]
        parts = exchange(pieces)
        size = grad.shape[1] // count
        if size % 128 == 0:
            return lay(count, me.reshape(1), parts)
        parts = [lax.select_n(me ^ place, *parts) for place in range(ways)]
        return jnp.concatenate(
            [part[:, n * size : (n + 1) * size] for n in range(count) for part in parts], axis=1
        ).astype(f32)

    small = (
        attention_gain,
        attention_shift,
        output_bias,
        feedforward_gain,
        feedforward_shift,
        contract_bias,
        query_value_bias,
        expand_bias,
    )
    every = range(ways)
    begin = (document_ids[0] - me_dp * length).reshape(-1, inner_slab)
    kinds, lines = len(small), begin.shape[0]
    begin = [*(begin >> 5).astype(bf16), *(begin & 31).astype(bf16)]
    qkv_parts = exchange(pieces_of(query_key_value, 3))
    out_block = jnp.concatenate([output_weight, pack([*small, *begin], width)], axis=0)
    out_parts = [out_block] + [
        lax.ppermute(out_block, "dp", [(d, (d + 2 * n) % groups) for d in range(groups)])
        for n in range(1, line)
    ]
    block = residual_in[0]
    qkv_parts, out_parts, expand_weight, block = lax.optimization_barrier(
        (qkv_parts, out_parts, expand_weight, block)
    )
    qkv_weight = gather_dp(place_parts(qkv_parts, 0))
    packs = [part[slab:, :inner_slab] for part in out_parts]
    packs = [lax.select_n((spot - n + line) % line, *packs) for n in range(line)]
    other = core_swap(jnp.concatenate(packs, axis=1))
    packed = []
    for n, mine in enumerate(packs):
        theirs = other[:, n * inner_slab : (n + 1) * inner_slab]
        packed += [jnp.where(core == 0, mine, theirs), jnp.where(core == 0, theirs, mine)]
    packed = jnp.concatenate(packed, axis=1)
    exp_parts = exchange(
        [jnp.concatenate([piece, packed], axis=0) for piece in pieces_of(expand_weight, groups)]
    )
    block_all = gather_rows(block)
    out_mine = jnp.concatenate(
        [
            lax.select_n((spot - n + line) % line, *[part[:slab] for part in out_parts])
            for n in range(line)
        ],
        axis=0,
    )
    block_all, exp_parts, out_mine = lax.optimization_barrier((block_all, exp_parts, out_mine))
    packs = [part[slab:] for part in exp_parts]
    exp_parts = [part[:slab] for part in exp_parts]
    begin = [
        lax.dynamic_slice_in_dim(part[kinds : kinds + 2 * lines], me_dp * inner_slab, inner_slab, 1)
        for part in packs
    ]
    begin = [32.0 * item[:lines].astype(f32) + item[lines:].astype(f32) for item in begin]
    starts = jnp.concatenate(begin, axis=0).astype(jnp.int32).reshape(length, 1)
    packed = [part[:kinds].astype(f32).reshape(kinds, groups, inner_slab) for part in packs]
    packed = jnp.stack([lax.select_n(me ^ place, *packed) for place in every], axis=2)
    whole = [packed[n, :, :, : item.shape[0]].reshape(-1) for n, item in enumerate(small)]
    att_gain, att_shift, out_bias, ff_gain, ff_shift, con_bias, qv_bias, exp_bias = whole
    exp_bias = lax.dynamic_index_in_dim(
        exp_bias.reshape(groups, ways, inner_slab), me, 1, keepdims=False
    ).reshape(-1)
    qv_bias = lax.dynamic_index_in_dim(qv_bias.reshape(2, ways, features), me, 1, keepdims=False)
    exp_weight = gather_dp(place_parts(exp_parts, 0))
    con_weight = gather_dp(contract_weight)
    out_near = gather_near(out_mine)
    grad_out = output_grad[0]
    slopes = jnp.exp2(
        -8.0 * ((me * heads + jnp.arange(heads, dtype=jnp.int32)).astype(f32) + 1.0) / HEADS
    )

    rows = block.astype(f32)
    unit_in, scale_in = unit_rows(rows)
    normed_low = (unit_rows(block_all.astype(f32))[0] * att_gain + att_shift).astype(bf16)
    bias = jnp.concatenate([qv_bias[0], jnp.zeros((features,), f32), qv_bias[1]])
    projected = (dot(normed_low, qkv_weight) + bias).astype(bf16)
    projected, out_near = lax.optimization_barrier((projected, out_near))
    out_all = gather_far(out_near)
    grad_near = gather_near(grad_out)
    me_array = me.reshape(1)
    attended, probs = attend_forward(stretch, me_array, slopes, starts, projected)
    attended, grad_near, out_all = lax.optimization_barrier((attended, grad_near, out_all))
    out_own = [
        jnp.concatenate([item.reshape(-1, slab, width) for item in out_all[2 * way : 2 * way + 2]])
        for way in every
    ]
    out_own = jnp.stack(out_own, axis=1).reshape(width // 2, width)
    out_other = core_swap(out_own)
    device = jnp.stack([me, core])
    rows_own, rows_other = arrange(
        slab, device, exchange([rows_of(attended, way) for way in every])
    )
    middle = rows + dot(rows_own, out_own) + dot(rows_other, out_other) + out_bias

    unit_mid, scale_mid = unit_rows(middle)
    normed_mid = gather_rows((unit_mid * ff_gain + ff_shift).astype(bf16))
    normed_mid, grad_near = lax.optimization_barrier((normed_mid, grad_near))
    grad_out_all = jnp.concatenate(gather_far(grad_near), axis=0)
    inner = dot(normed_mid, exp_weight) + exp_bias
    cumulative = (1.0 + lax.erf(inner * 0.7071067811865476)) * 0.5
    active = (inner * cumulative).astype(bf16)
    con_term = dot(active, grad_out_all, ((0,), (0,))).astype(bf16)
    con_term, con_weight = lax.optimization_barrier((con_term, con_weight))
    con_sum = scatter_dp(con_term)
    grad_active = dot(grad_out_all, con_weight, ((1,), (1,)))
    density = jnp.exp(-0.5 * inner * inner) * 0.3989422804014327
    grad_inner = (grad_active * (cumulative + inner * density)).astype(bf16)
    far, near = split_rows(grad_inner, exp_weight, ((1,), (1,)))
    exp_term = dot(normed_mid, grad_inner, ((0,), (0,))).astype(bf16)
    exp_bias_term = jnp.sum(grad_inner.astype(f32), axis=0)
    grad_normed_mid = scatter_rows(far, near)
    exp_term, grad_normed_mid = lax.optimization_barrier((exp_term, grad_normed_mid))
    exp_sum = scatter_dp(exp_term)
    grad_mid_norm, ff_gain_term, ff_shift_term = norm_backward(
        grad_normed_mid, unit_mid, scale_mid, ff_gain
    )
    grad_out_full = grad_out.astype(f32)
    grad_middle = grad_out_full + grad_mid_norm
    grad_branch = grad_middle.astype(bf16)

    grad_own = dot(grad_branch, out_own, ((1,), (1,)))
    grad_other = dot(grad_branch, out_other, ((1,), (1,)))
    grad_heads = disarrange(slab, device, grad_own, grad_other, ways)
    grad_heads, active, grad_branch = lax.optimization_barrier((grad_heads, active, grad_branch))
    grad_heads = jnp.concatenate(exchange(grad_heads), axis=0)
    give = dot(rows_other, grad_branch, ((0,), (0,))).astype(bf16)
    result = dot(active, con_weight)
    out_term = dot(rows_own, grad_branch, ((0,), (0,))) + core_swap(give).astype(f32)
    grad_heads, out_term, result = lax.optimization_barrier((grad_heads, out_term, result))
    last = (ways - 1) * stretch
    result_first = (scatter_far(result[last:]), scatter_side(result[:last]))
    out_term = out_term.reshape(line, ways, slab, width)
    out_term = [out_term[:, way].reshape(line * slab, width) for way in every]
    out_near = jnp.concatenate(out_term[:-1], axis=0)
    out_first = (scatter_far(out_term[-1]), scatter_side(out_near))
    grad_projected = jnp.concatenate(
        attend_backward(stretch, me_array, probs, projected, grad_heads), axis=1
    )
    qkv_term = dot(normed_low, grad_projected, ((0,), (0,))).astype(bf16)
    qkv_term, con_sum, grad_projected, out_first = lax.optimization_barrier(
        (qkv_term, con_sum, grad_projected, out_first)
    )
    far = dot(grad_projected[last:], qkv_weight, ((1,), (1,))).astype(bf16)
    far, grad_projected = lax.optimization_barrier((far, grad_projected))
    near = dot(grad_projected[:last], qkv_weight, ((1,), (1,)))
    first = (scatter_far(far), scatter_side(near))
    first, out_first, result_first, exp_sum = lax.optimization_barrier(
        (first, out_first, result_first, exp_sum)
    )
    exp_grad = own_rows(exp_sum, groups)
    grad_normed_in = scatter_near(near, *first)
    out_term = scatter_near(out_near, *out_first).astype(bf16)
    result = scatter_near(result[:last], *result_first)
    layer_output = (middle + result + con_bias).astype(bf16)[None]
    qkv_sum = scatter_dp(qkv_term)
    grad_normed_in, qkv_sum = lax.optimization_barrier((grad_normed_in, qkv_sum))
    grad_in_norm, att_gain_term, att_shift_term = norm_backward(
        grad_normed_in, unit_in, scale_in, att_gain
    )
    input_grad = (grad_middle + grad_in_norm).astype(bf16)[None]

    bias_sums = jnp.sum(grad_projected.astype(f32), axis=0).reshape(3, features)
    qv_term = lax.dynamic_update_slice(
        jnp.zeros((2, ways, features), f32),
        jnp.stack([bias_sums[0], bias_sums[2]])[:, None],
        (0, me, 0),
    ).reshape(-1)
    exp_term = lax.dynamic_update_slice(
        jnp.zeros((groups, ways, inner_slab), f32),
        exp_bias_term.reshape(groups, 1, inner_slab),
        (0, me, 0),
    ).reshape(-1)
    terms = (
        att_gain_term,
        att_shift_term,
        jnp.sum(grad_branch.astype(f32), axis=0),
        ff_gain_term,
        ff_shift_term,
        jnp.sum(grad_out_full, axis=0),
        qv_term,
        exp_term,
    )
    count = groups * ways
    sums = jnp.concatenate([item.reshape(count, -1) for item in terms], axis=1)
    out_grad = halving(out_term.reshape(line, slab, width), "dp", bits_of(groups)[:0:-1])
    out_grad = out_grad[0].astype(f32)
    sums = halving(sums, "dp", bits_of(groups)[::-1])
    sums = halving(sums, "ctx", bits_of(ways)[::-1]).reshape(-1)
    qkv_grad = own_rows(qkv_sum, 3)
    own, at = [], 0
    for item in small:
        own.append(sums[at : at + item.shape[0]])
        at += item.shape[0]
    return (
        layer_output,
        input_grad,
        own[0],
        own[1],
        qkv_grad,
        own[6],
        out_grad,
        own[2],
        own[3],
        own[4],
        exp_grad,
        own[7],
        con_sum.astype(f32),
        own[5],
    )


def solution(mesh):
    tokens = P("dp", "ctx", None)
    vector = P(ALL)
    matrix = P(ALL, None)
    in_specs = (
        tokens,
        P("dp", "ctx"),
        vector,
        vector,
        matrix,
        vector,
        matrix,
        vector,
        vector,
        vector,
        matrix,
        vector,
        matrix,
        vector,
        tokens,
    )
    out_specs = (
        tokens,
        tokens,
        vector,
        vector,
        matrix,
        vector,
        matrix,
        vector,
        vector,
        vector,
        matrix,
        vector,
        matrix,
        vector,
    )
    return jax.shard_map(shards, mesh=mesh, in_specs=in_specs, out_specs=out_specs, check_vma=False)
```
